128 devices in a mesh: batch: 8 (over x_lo, y), lat: 16 (over x_hi, z, core).
Axes of the slice: x: 4 (x_hi: 2, x_lo: 2; x = x_hi * 2 + x_lo), y: 4, z: 4, core: 2. Of those that a mesh axis runs over, the one named last changes fastest.
Arguments:
- field: bfloat16 [16, 96, 180, 768], P('batch', 'lat'), may hold values from -6 to 6
- cotangent: bfloat16 [16, 96, 180, 768], P('batch', 'lat'), may hold values from -6 to 6
- weight_one: float32 [2, 8, 96, 96], replicated, may hold values from -0.4375 to 0.4375
- bias_one: float32 [2, 8, 96], replicated, may hold values from -2 to 2
- weight_two: float32 [2, 8, 96, 96], replicated, may hold values from -0.4375 to 0.4375
- bias_two: float32 [2, 8, 96], replicated, may hold values from -2 to 2
Outputs:
- field_grad: bfloat16 [16, 96, 180, 768], P('batch', 'lat')
- weight_one_grad: float32 [2, 8, 96, 96], replicated
- bias_one_grad: float32 [2, 8, 96], replicated
- weight_two_grad: float32 [2, 8, 96, 96], replicated
- bias_two_grad: float32 [2, 8, 96], replicated
The draws below stay inside these ranges and needn't reach their ends.
All inputs are finite; a program needn't handle non-finite values.
Results may differ from the reference program's by a relative error of at most 0.017.
Values may be sent and summed in bfloat16 or wider, within the bound.
A program may use at most 192 MiB of HBM per device.

```python
import math
import jax
import jax.numpy as jnp
from jax import lax

C = 768
NB = 8
W = 180
LAT = 96
KP = 96
BS = 96
SAMPLES = 16


def block_levels(key, dims, cuts, smallest, top_value):
    gain, own = 1.0, jax.random.fold_in(key, 6)
    for position, shards_of in cuts:
        draws = jnp.exp(jax.random.uniform(jax.random.fold_in(own, position), (shards_of,), jnp.float32, smallest / len(cuts), top_value / len(cuts)))
        gain = gain * jnp.repeat(draws, dims[position] // shards_of).reshape([-1 if axis == position else 1 for axis in range(len(dims))])
    return gain


def noise(stream_key, shape, deviation, reach, split=(), kind=jnp.bfloat16):
    values = jax.random.normal(stream_key, shape, jnp.float32) * deviation
    if len(split) > 0:
        values = block_levels(stream_key, shape, split, -0.22, 0.18) * values
    return jnp.clip(values, min=-reach, max=reach).astype(kind)


def setup_inputs(seed: int = 0) -> dict:
    seeds = jax.random.split(jax.random.key(seed), 7)
    field = noise(seeds[0], (SAMPLES, LAT, W, C), 1.0, 6.0, ((0, 8), (1, 16)))
    cotangent = noise(seeds[1], (SAMPLES, LAT, W, C), 1.0, 6.0, ((0, 8), (1, 16)))
    weight_one = noise(seeds[2], (2, NB, BS, BS), (2 * BS) ** -0.5, 0.4375, (), jnp.float32)
    bias_one = noise(seeds[3], (2, NB, BS), 0.3, 2.0, (), jnp.float32)
    weight_two = noise(seeds[4], (2, NB, BS, BS), (2 * BS) ** -0.5, 0.4375, (), jnp.float32)
    bias_two = noise(seeds[5], (2, NB, BS), 0.3, 2.0, (), jnp.float32)
    return {"field": field, "cotangent": cotangent, "weight_one": weight_one, "bias_one": bias_one, "weight_two": weight_two, "bias_two": bias_two}


shrink_width = 0.25

def lon_tables(width, slots):
    wpos = jnp.arange(width, dtype=jnp.int32)
    kpos = jnp.arange(slots, dtype=jnp.int32)
    phase = wpos[:, None] * kpos[None, :] % width
    angle = phase.astype(jnp.float32) * (2.0 * math.pi / width)
    valid = (kpos <= width // 2).astype(jnp.float32)[None, :]
    factor = 1.0 / math.sqrt(width)
    cosine = jnp.cos(angle) * valid * factor
    sine = jnp.sin(angle) * valid * factor
    forward = jnp.stack([cosine, -sine], axis=1).astype(jnp.bfloat16)
    weight = jnp.where((kpos == 0) | (kpos == width // 2), 1.0, 2.0).astype(jnp.float32)[None, :]
    inverse = jnp.stack([(cosine * weight).T, (-sine * weight).T], axis=0).astype(jnp.bfloat16)
    return (forward, inverse)

def lat_table(count, sign):
    pos = jnp.arange(count, dtype=jnp.int32)
    phase = pos[:, None] * pos[None, :] % count
    angle = phase.astype(jnp.float32) * (2.0 * math.pi / count)
    factor = 1.0 / math.sqrt(count)
    cosine = jnp.cos(angle) * factor
    sine = jnp.sin(angle) * (factor * sign)
    upper = jnp.stack([cosine, -sine], axis=-1)
    lower = jnp.stack([sine, cosine], axis=-1)
    return jnp.stack([upper, lower], axis=1).astype(jnp.bfloat16)

def block_matrix(weights):
    real_part = weights[0]
    imag_part = weights[1]
    first = jnp.stack([real_part, imag_part], axis=2)
    second = jnp.stack([-imag_part, real_part], axis=2)
    return jnp.stack([first, second], axis=0)

def spectral_mix(spectra, weight_one, bias_one, weight_two, bias_two, lat_fwd, lat_inv):
    samples, lats, _, slots, chans = spectra.shape
    blocks = bias_one.shape[1]
    size = bias_one.shape[2]
    mixed = jnp.einsum('mphq,bhqkc->bmpkc', lat_fwd, spectra, preferred_element_type=jnp.float32)
    mixed = mixed.reshape(samples, lats, 2, slots, blocks, size)
    first = jnp.einsum('bmqkni,qnipj->bmpknj', mixed, block_matrix(weight_one), precision=lax.Precision.HIGHEST)
    first = first + bias_one[None, None, :, None, :, :]
    hidden = jax.nn.gelu(first, approximate=True)
    second = jnp.einsum('bmqkni,qnipj->bmpknj', hidden, block_matrix(weight_two), precision=lax.Precision.HIGHEST)
    second = second + bias_two[None, None, :, None, :, :]
    shrunk = second - shrink_width * jnp.tanh(second / shrink_width)
    shrunk = shrunk.reshape(samples, lats, 2, slots, chans).astype(jnp.bfloat16)
    result = jnp.einsum('hpmq,bmqkc->bhpkc', lat_inv, shrunk, preferred_element_type=jnp.float32)
    return result.astype(jnp.bfloat16)

def reference(field, cotangent, weight_one, bias_one, weight_two, bias_two):
    samples, lats, width, chans = field.shape
    lon_fwd, lon_inv = lon_tables(width, KP)
    lat_fwd = lat_table(lats, -1.0)
    lat_inv = lat_table(lats, 1.0)

    def one_sample(carry, pair):
        sample_field, sample_cot = pair
        spectra = jnp.einsum('wqk,bhwc->bhqkc', lon_fwd, sample_field[None], preferred_element_type=jnp.float32).astype(jnp.bfloat16)
        spec_cot = jnp.einsum('qkw,bhwc->bhqkc', lon_inv, sample_cot[None], preferred_element_type=jnp.float32).astype(jnp.bfloat16)

        def mixing(spec, first_w, first_b, second_w, second_b):
            return spectral_mix(spec, first_w, first_b, second_w, second_b, lat_fwd, lat_inv)
        _, pullback = jax.vjp(mixing, spectra, weight_one, bias_one, weight_two, bias_two)
        grads = pullback(spec_cot)
        field_part = jnp.einsum('wqk,bhqkc->bhwc', lon_fwd, grads[0], preferred_element_type=jnp.float32).astype(jnp.bfloat16)
        carry = (carry[0] + grads[1], carry[1] + grads[2], carry[2] + grads[3], carry[3] + grads[4])
        return (carry, field_part[0])
    start = (jnp.zeros(weight_one.shape, jnp.float32), jnp.zeros(bias_one.shape, jnp.float32), jnp.zeros(weight_two.shape, jnp.float32), jnp.zeros(bias_two.shape, jnp.float32))
    totals, field_grad = lax.scan(one_sample, start, (field, cotangent))
    factor = 1.0 / math.sqrt(samples * lats * (width // 2 + 1))
    return (field_grad, totals[0] * factor, totals[1] * factor, totals[2] * factor, totals[3] * factor)
```

```python
import functools
import math

import jax
import jax.numpy as jnp
import numpy as np
from jax import lax
from jax.experimental import pallas as pl
from jax.experimental.pallas import tpu as pltpu
from jax.sharding import PartitionSpec as P

MESH = pl.DeviceIdType.MESH
F32, BF16 = jnp.float32, jnp.bfloat16
KP = 96
QUARTER = 24
JB = 8
CHUNKS = QUARTER // JB
HALF = 384
TILES = HALF // 128
LOCAL = 6
SAMPLES = 2
LAT = 96
WIDTH = 180
CH = 768
BS = 96
ROWS = JB * LAT
RB = ROWS // 2
OFFSETS = [(dx, dz, dc) for dx in (1, 0) for dz in (2, 1, 3, 0) for dc in (0, 1)]
WIN = [(0, 512), (0, 768), (256, 768)]
PIECES = [[(0, 0, 96)], [(0, 96, 128), (1, 0, 64)], [(1, 64, 128), (2, 0, 32)], [(2, 32, 128)]]


def lon_tables():
    wpos, kpos = np.arange(WIDTH), np.arange(KP)
    angle = (wpos[:, None] * kpos[None, :] % WIDTH).astype(np.float32) * np.float32(2.0 * math.pi / WIDTH)
    valid = (kpos <= WIDTH // 2).astype(np.float32)[None, :]
    factor = np.float32(1.0 / math.sqrt(WIDTH))
    cosine, sine = np.cos(angle) * valid * factor, np.sin(angle) * valid * factor
    weight = np.where((kpos == 0) | (kpos == WIDTH // 2), 1.0, 2.0).astype(np.float32)[None, :]

    def rows(real, imag):
        both = np.stack([real.T, imag.T]).reshape(2, 4, CHUNKS, JB, WIDTH)
        return both.transpose(1, 2, 0, 3, 4).reshape(2 * KP, WIDTH).astype(BF16)

    return rows(cosine, -sine), rows(cosine * weight, -sine * weight)


def lat_tables():
    pos = np.arange(LAT)
    angle = (pos[:, None] * pos[None, :] % LAT).astype(np.float32) * np.float32(2.0 * math.pi / LAT)
    factor = np.float32(1.0 / math.sqrt(LAT))
    cosine = np.cos(angle) * factor

    def real_form(sign):
        sine = np.sin(angle) * np.float32(factor * sign)
        return np.stack([np.stack([cosine, -sine], -1), np.stack([sine, cosine], -1)], 1).astype(BF16)

    fwd = real_form(-1.0).transpose(1, 0, 3, 2).reshape(2 * LAT, 2 * LAT)
    inv = real_form(1.0).transpose(3, 2, 1, 0).reshape(2 * LAT, 2 * LAT)
    return fwd, inv, np.ascontiguousarray(fwd.T)


def dot(a, b):
    return jnp.dot(a, b, preferred_element_type=F32)


def dot_tb(a, b):
    return lax.dot_general(a, b, (((1,), (1,)), ((), ())), preferred_element_type=F32)


def dot_ta(a, b):
    return lax.dot_general(a, b, (((0,), (0,)), ((), ())), preferred_element_type=F32)


def kernel(
    field, cot, w1, b1, w2, b2, tf, ti, tt, l1, l2, l3,
    out, gout,
    slab, send, recv, gsend, grecv, mixed, hidden, slope, mask, dsec, dfir, scr, bmat, wm, wtmp, bias, acc, gb,
    wraw, braw, slab_sem, out_sem, par_sem, ssem, rsem, own_sem,
):
    batch, me = lax.axis_index("batch"), lax.axis_index("lat")
    half, zz, core = me // 8, (me // 2) % 4, me % 2

    def partner(o):
        dx, dz, dc = o
        return (half + dx) % 2, (zz + dz) % 4, (core + dc) % 2

    def index(part):
        return part[0] * 8 + part[1] * 2 + part[2]

    def source(o):
        dx, dz, dc = o
        return ((half + dx) % 2) * 8 + ((zz + 4 - dz) % 4) * 2 + (core + dc) % 2

    def slab_copy(ref, s, h):
        return pltpu.make_async_copy(ref.at[s, h], slab.at[s * LOCAL + h], slab_sem.at[s * LOCAL + h])

    for s in range(SAMPLES):
        for h in range(LOCAL):
            slab_copy(field, s, h).start()
    params = [
        pltpu.make_async_copy(w1.at[:, pl.ds(half * 4, 4)], wraw.at[0], par_sem.at[0]),
        pltpu.make_async_copy(w2.at[:, pl.ds(half * 4, 4)], wraw.at[1], par_sem.at[1]),
        pltpu.make_async_copy(b1, braw.at[0], par_sem.at[2]),
        pltpu.make_async_copy(b2, braw.at[1], par_sem.at[3]),
    ]
    for copy in params:
        copy.start()

    barrier = pltpu.get_barrier_semaphore()
    for o in OFFSETS:
        if o != (0, 0, 0):
            pl.semaphore_signal(barrier, inc=1, device_id=(batch, index(partner(o))), device_id_type=MESH)

    def lanes(part):
        return pl.ds(pl.multiple_of(part * HALF, 128), HALF)

    def rows16(quarter, jc):
        return pl.ds(pl.multiple_of(quarter * 48 + jc * 16, 16), 16)

    def chunk(jc):
        return pl.ds(pl.multiple_of(jc * 16, 16), 16)

    def inward(a, jc, i):
        to = partner(OFFSETS[i])
        src = send.at[a, to[2], :, rows16(to[1], jc), lanes(to[0])]
        dst = recv.at[a, me, :, chunk(jc), :]
        if OFFSETS[i] == (0, 0, 0):
            return pltpu.make_async_copy(src, dst, own_sem.at[a, jc])
        return pltpu.make_async_remote_copy(
            src, dst, ssem.at[a, jc, i], rsem.at[a, jc, i], device_id=(batch, index(to)), device_id_type=MESH
        )

    def inward_wait(a, jc, i):
        if OFFSETS[i] == (0, 0, 0):
            inward(a, jc, i).wait()
            return
        dst = recv.at[a, source(OFFSETS[i]), :, chunk(jc), :]
        pltpu.make_async_remote_copy(
            dst, dst, ssem.at[a, jc, i], rsem.at[a, jc, i], device_id=(batch, me), device_id_type=MESH
        ).wait_recv()

    def outward(jc, i):
        to = index(partner(OFFSETS[i]))
        src = gsend.at[pl.ds(to * LOCAL, LOCAL), chunk(jc), :]
        dst = grecv.at[core, :, rows16(zz, jc), lanes(half)]
        if OFFSETS[i] == (0, 0, 0):
            return pltpu.make_async_copy(src, dst, own_sem.at[2, jc])
        return pltpu.make_async_remote_copy(
            src, dst, ssem.at[2, jc, i], rsem.at[2, jc, i], device_id=(batch, to), device_id_type=MESH
        )

    def outward_wait(jc, i):
        if OFFSETS[i] == (0, 0, 0):
            outward(jc, i).wait()
            return
        dx, dz, dc = OFFSETS[i]
        fx, fz, fc = (half + dx) % 2, (zz + 4 - dz) % 4, (core + dc) % 2
        dst = grecv.at[fc, :, rows16(fz, jc), lanes(fx)]
        pltpu.make_async_remote_copy(
            dst, dst, ssem.at[2, jc, i], rsem.at[2, jc, i], device_id=(batch, me), device_id_type=MESH
        ).wait_recv()

    def longitude(a, s):
        table = (tf, ti)[a]
        ref = (field, cot)[a]

        def one(h, carry):
            slab_copy(ref, s, h).wait()
            send[a, s, h] = dot(table[...], slab[s * LOCAL + h]).astype(BF16)
            if a == 0:
                slab_copy(cot, s, h).start()
            return carry

        lax.fori_loop(0, LOCAL, one, 0)

    def to_sample(a, jc, s):
        for i, o in enumerate(OFFSETS):

            @pl.when((core + o[2]) % 2 == s)
            def _(i=i):
                inward(a, jc, i).start()

    longitude(0, 0)
    pl.semaphore_wait(barrier, len(OFFSETS) - 1)
    to_sample(0, 0, 0)
    longitude(0, 1)
    to_sample(0, 0, 1)
    for jc in range(1, CHUNKS):
        for i in range(len(OFFSETS)):
            inward(0, jc, i).start()
    longitude(1, 0)
    longitude(1, 1)
    for jc in range(CHUNKS):
        for i in range(len(OFFSETS)):
            inward(1, jc, i).start()

    for copy in params:
        copy.wait()
    row_id = lax.broadcasted_iota(jnp.int32, (BS, HALF), 0)
    col_id = lax.broadcasted_iota(jnp.int32, (BS, HALF), 1)
    for w in range(2):
        for part in range(2):
            total = jnp.zeros((8, HALF), F32)
            for n in range(4):
                place = jnp.where(row_id + n * BS == col_id, 1.0, 0.0).astype(F32)
                placed = dot(wraw[w, part, n].astype(BF16), place.astype(BF16))
                wtmp[part, n * BS : (n + 1) * BS, :] = placed.astype(BF16)
                line = jnp.broadcast_to(braw[w, part, pl.ds(half * 4 + n, 1), :], (8, BS))
                total = total + jnp.dot(line, place, precision=lax.Precision.HIGHEST, preferred_element_type=F32)
            for t in range(TILES):
                c = (2 * t + part) * 128
                bias[w, :, c : c + 128] = total[:, t * 128 : (t + 1) * 128]
        for t in range(TILES):
            for u in range(TILES):
                real = wtmp[0, t * 128 : (t + 1) * 128, u * 128 : (u + 1) * 128]
                imag = wtmp[1, t * 128 : (t + 1) * 128, u * 128 : (u + 1) * 128]
                r, c = t * 256, u * 256
                wm[w, r : r + 128, c : c + 128] = real
                wm[w, r : r + 128, c + 128 : c + 256] = imag
                wm[w, r + 128 : r + 256, c : c + 128] = -imag
                wm[w, r + 128 : r + 256, c + 128 : c + 256] = real
    acc[...] = jnp.zeros_like(acc)
    gb[...] = jnp.zeros_like(gb)

    def gather(a, jc):
        for i in range(len(OFFSETS)):
            inward_wait(a, jc, i)

        def one(l, carry):
            rows = recv[a, l, :, chunk(jc), :].astype(F32).reshape(LOCAL * 16, HALF)
            for t in range(TILES):
                scr[t, pl.ds(pl.multiple_of(l * 96, 8), 96), :] = rows[:, t * 128 : (t + 1) * 128]
            return carry

        lax.fori_loop(0, 16, one, 0)

    def column(j):
        parts = [
            jnp.concatenate([scr[t, pl.ds(q * JB + j, LAT, stride=16), :] for t in range(TILES)], axis=1)
            for q in range(2)
        ]
        return jnp.concatenate(parts, axis=0).astype(BF16)

    def row_block(jc, rb):
        return pl.ds(pl.multiple_of(jc * ROWS + rb * RB, 128), RB)

    def forward(jc, carry):
        gather(0, jc)

        def one(j, c):
            res = dot(l1[...], column(j))
            rows = pl.ds(pl.multiple_of(jc * ROWS + j * LAT, 32), LAT)
            for p in range(2):
                for t in range(TILES):
                    mixed[rows, (2 * t + p) * 128 : (2 * t + p + 1) * 128] = res[
                        p * LAT : (p + 1) * LAT, t * 128 : (t + 1) * 128
                    ].astype(BF16)
            return c

        lax.fori_loop(0, JB, one, 0)

        def mix(rb, c):
            rows = row_block(jc, rb)
            for t in range(TILES):
                lo, hi = WIN[t]
                cols = slice(t * 256, (t + 1) * 256)
                x = dot(mixed[rows, lo:hi], wm[0, lo:hi, cols]) + bias[0, 0:1, cols]
                c0, c1 = math.sqrt(2.0 / math.pi), 0.044715
                xx = x * x
                th = jnp.tanh(x * (c0 + (c0 * c1) * xx))
                gate = 0.5 + 0.5 * th
                hidden[rows, cols] = (x * gate).astype(BF16)
                rise = (0.5 * x) * (1.0 - th * th) * (c0 + (3.0 * c0 * c1) * xx)
                slope[rows, cols] = (gate + rise).astype(BF16)
            for t in range(TILES):
                lo, hi = WIN[t]
                cols = slice(t * 256, (t + 1) * 256)
                y = dot(hidden[rows, lo:hi], wm[1, lo:hi, cols]) + bias[1, 0:1, cols]
                th = jnp.tanh(4.0 * y)
                mask[rows, cols] = (th * th).astype(BF16)
            return c

        lax.fori_loop(0, 2, mix, 0)
        return carry

    lax.fori_loop(0, CHUNKS, forward, 0)

    def backward(jc, carry):
        gather(1, jc)

        def one(j, c):
            res = dot(l2[...], column(j)).astype(BF16)
            rows = pl.ds(pl.multiple_of(jc * ROWS + j * LAT, 32), LAT)
            here = pl.ds(pl.multiple_of(j * LAT, 32), LAT)
            for p in range(2):
                for t in range(TILES):
                    cols = slice((2 * t + p) * 128, (2 * t + p + 1) * 128)
                    part = res[p * LAT : (p + 1) * LAT, t * 128 : (t + 1) * 128].astype(F32)
                    dsec[here, cols] = (part * mask[rows, cols].astype(F32)).astype(BF16)
            return c

        lax.fori_loop(0, JB, one, 0)

        def mix(rb, c):
            rows = row_block(jc, rb)
            here = pl.ds(pl.multiple_of(rb * RB, 128), RB)
            for t in range(TILES):
                lo, hi = WIN[t]
                cols = slice(t * 256, (t + 1) * 256)
                d = dot_tb(dsec[here, lo:hi], wm[1, cols, lo:hi])
                dfir[here, cols] = (d * slope[rows, cols].astype(F32)).astype(BF16)
            for t in range(TILES):
                lo, hi = WIN[t]
                cols = slice(t * 256, (t + 1) * 256)
                d = dot_tb(dfir[here, lo:hi], wm[0, cols, lo:hi]).astype(BF16)
                for jl in range(JB // 2):
                    for p in range(2):
                        bmat[rb * (JB // 2) + jl, p * LAT : (p + 1) * LAT, t * 128 : (t + 1) * 128] = d[
                            jl * LAT : (jl + 1) * LAT, p * 128 : (p + 1) * 128
                        ]
            return c

        lax.fori_loop(0, 2, mix, 0)

        def last(j, c):
            res = dot(l3[...], bmat[j])
            for q in range(2):
                for t in range(TILES):
                    scr[t, pl.ds(q * JB + j, LAT, stride=16), :] = res[
                        q * LAT : (q + 1) * LAT, t * 128 : (t + 1) * 128
                    ]
            return c

        lax.fori_loop(0, JB, last, 0)

        def pack(l, c):
            for t in range(TILES):
                part = scr[t, pl.ds(pl.multiple_of(l * 96, 8), 96), :]
                gsend[pl.ds(l * LOCAL, LOCAL), chunk(jc), t * 128 : (t + 1) * 128] = part.astype(BF16).reshape(
                    LOCAL, 16, 128
                )
            return c

        lax.fori_loop(0, 16, pack, 0)
        for i in range(len(OFFSETS)):
            outward(jc, i).start()

        here = pl.ds(pl.multiple_of(jc * ROWS, 128), ROWS)
        for t in range(TILES):
            lo, hi = WIN[t]
            cols = slice(t * 256, (t + 1) * 256)
            acc[1, cols, lo:hi] += dot_ta(hidden[here, cols], dsec[:, lo:hi])
            acc[0, cols, lo:hi] += dot_ta(mixed[here, cols], dfir[:, lo:hi])
        ones = jnp.ones((16, ROWS), BF16)
        gb[0] += dot(ones, dfir[...])[0:8]
        gb[1] += dot(ones, dsec[...])[0:8]
        return carry

    lax.fori_loop(0, CHUNKS, backward, 0)

    for w in range(2):
        for n in range(4):
            first, last_ = PIECES[n][0][0], PIECES[n][-1][0]
            shift = PIECES[n][0][1]

            def window(get):
                wide = jnp.concatenate([get(first), get(last_)], axis=1)
                return pltpu.roll(wide, (256 - shift) % 256, 1)[:, 0:128]

            for part in range(2):

                def block(u):
                    pieces = []
                    for t, lo, hi in PIECES[n]:
                        r, c = t * 256, u * 256
                        top = acc[w, r + lo : r + hi, c + part * 128 : c + (part + 1) * 128]
                        low = acc[w, r + 128 + lo : r + 128 + hi, c + (1 - part) * 128 : c + (2 - part) * 128]
                        pieces.append(top + low if part == 0 else top - low)
                    return pieces[0] if len(pieces) == 1 else jnp.concatenate(pieces, axis=0)

                b = (w * 2 + part) * 4 + n
                gout[b, 0:BS, :] = window(block)
                gout[b, BS : BS + 8, :] = window(lambda u: gb[w, :, (2 * u + part) * 128 : (2 * u + part + 1) * 128])

    for jc in range(CHUNKS):
        for i in range(len(OFFSETS)):
            outward_wait(jc, i)

    def final(h, carry):
        for s in range(SAMPLES):
            slab[s * LOCAL + h] = dot(tt[...], grecv[s, h]).astype(BF16)
            pltpu.make_async_copy(slab.at[s * LOCAL + h], out.at[s, h], out_sem.at[s * LOCAL + h]).start()
        return carry

    lax.fori_loop(0, LOCAL, final, 0)
    for a in range(3):
        for jc in range(CHUNKS):
            for i, o in enumerate(OFFSETS):
                if o != (0, 0, 0):
                    (outward(jc, i) if a == 2 else inward(a, jc, i)).wait_send()
    for s in range(SAMPLES):
        for h in range(LOCAL):
            pltpu.make_async_copy(slab.at[s * LOCAL + h], out.at[s, h], out_sem.at[s * LOCAL + h]).wait()


def local(field, cotangent, weight_one, bias_one, weight_two, bias_two):
    tf, ti = lon_tables()
    tt = np.ascontiguousarray(tf.T)
    l1, l2, l3 = lat_tables()
    hbm, vmem = pl.BlockSpec(memory_space=pl.ANY), pl.BlockSpec(memory_space=pltpu.VMEM)
    n_off = len(OFFSETS)
    field_grad, blocks = pl.pallas_call(
        kernel,
        name="afno_backward",
        out_shape=(
            jax.ShapeDtypeStruct(field.shape, BF16),
            jax.ShapeDtypeStruct((16, BS + 8, 128), F32),
        ),
        in_specs=[hbm] * 6 + [vmem] * 6,
        out_specs=(hbm, vmem),
        scratch_shapes=[
            pltpu.VMEM((SAMPLES * LOCAL, WIDTH, CH), BF16),
            pltpu.VMEM((2, SAMPLES, LOCAL, 2 * KP, CH), BF16),
            pltpu.VMEM((2, 16, LOCAL, 2 * QUARTER, HALF), BF16),
            pltpu.VMEM((LAT, 2 * QUARTER, HALF), BF16),
            pltpu.VMEM((SAMPLES, LOCAL, 2 * KP, CH), BF16),
            pltpu.VMEM((CHUNKS * ROWS, CH), BF16),
            pltpu.VMEM((CHUNKS * ROWS, CH), BF16),
            pltpu.VMEM((CHUNKS * ROWS, CH), BF16),
            pltpu.VMEM((CHUNKS * ROWS, CH), BF16),
            pltpu.VMEM((ROWS, CH), BF16),
            pltpu.VMEM((ROWS, CH), BF16),
            pltpu.VMEM((TILES, LAT * 16, 128), F32),
            pltpu.VMEM((JB, 2 * LAT, HALF), BF16),
            pltpu.VMEM((2, CH, CH), BF16),
            pltpu.VMEM((2, HALF, HALF), BF16),
            pltpu.VMEM((2, 8, CH), F32),
            pltpu.VMEM((2, CH, CH), F32),
            pltpu.VMEM((2, 8, CH), F32),
            pltpu.VMEM((2, 2, 4, BS, BS), F32),
            pltpu.VMEM((2, 2, 8, BS), F32),
            pltpu.SemaphoreType.DMA((SAMPLES * LOCAL,)),
            pltpu.SemaphoreType.DMA((SAMPLES * LOCAL,)),
            pltpu.SemaphoreType.DMA((4,)),
            pltpu.SemaphoreType.DMA((3, CHUNKS, n_off)),
            pltpu.SemaphoreType.DMA((3, CHUNKS, n_off)),
            pltpu.SemaphoreType.DMA((3, CHUNKS)),
        ],
        compiler_params=pltpu.CompilerParams(
            collective_id=0, has_side_effects=True, vmem_limit_bytes=62 * 1024 * 1024
        ),
        cost_estimate=pl.CostEstimate(flops=10**10, bytes_accessed=10**7, transcendentals=4 * 10**6),
    )(field, cotangent, weight_one, bias_one, weight_two, bias_two, tf, ti, tt, l1, l2, l3)

    half = lax.axis_index("lat") // 8
    spread = jnp.zeros((2,) + blocks.shape, F32)
    spread = lax.dynamic_update_slice(spread, blocks[None], (half, 0, 0, 0))
    total_samples = SAMPLES * lax.axis_size("batch")
    factor = 1.0 / math.sqrt(total_samples * LAT * (WIDTH // 2 + 1))
    total = lax.psum(spread, ("batch", "lat")) * factor
    total = total.reshape(2, 2, 2, 4, BS + 8, 128)[..., :BS].transpose(1, 2, 0, 3, 4, 5).reshape(2, 2, 8, BS + 8, BS)
    return field_grad, total[0, :, :, :BS], total[0, :, :, BS], total[1, :, :, :BS], total[1, :, :, BS]


def solution(mesh):
    in_specs = (P("batch", "lat", None, None), P("batch", "lat", None, None), P(), P(), P(), P())
    out_specs = (P("batch", "lat", None, None), P(), P(), P(), P())
    return jax.shard_map(local, mesh=mesh, in_specs=in_specs, out_specs=out_specs, check_vma=False)
```

```python
import functools
import math

import jax
import jax.numpy as jnp
import numpy as np
from jax import lax
from jax.experimental import pallas as pl
from jax.experimental.pallas import tpu as pltpu
from jax.sharding import PartitionSpec as P

MESH = pl.DeviceIdType.MESH
F32, BF16 = jnp.float32, jnp.bfloat16
BATCH = 8
UNITS = 5
KP = 96
QUARTER = 24
JB = 8
CHUNKS = QUARTER // JB
HALF = 384
TILES = HALF // 128
LOCAL = 6
SAMPLES = 2
LAT = 96
WIDTH = 180
CH = 768
BS = 96
ROWS = JB * LAT
RB = ROWS // 2
OFFSETS = [(dx, dz, dc) for dx in (1, 0) for dz in (2, 1, 3, 0) for dc in (0, 1)]
WIN = [(0, 512), (0, 768), (256, 768)]
PIECES = [[(0, 0, 96)], [(0, 96, 128), (1, 0, 64)], [(1, 64, 128), (2, 0, 32)], [(2, 32, 128)]]


def lon_tables():
    wpos, kpos = np.arange(WIDTH), np.arange(KP)
    angle = (wpos[:, None] * kpos[None, :] % WIDTH).astype(np.float32) * np.float32(2.0 * math.pi / WIDTH)
    valid = (kpos <= WIDTH // 2).astype(np.float32)[None, :]
    factor = np.float32(1.0 / math.sqrt(WIDTH))
    cosine, sine = np.cos(angle) * valid * factor, np.sin(angle) * valid * factor
    weight = np.where((kpos == 0) | (kpos == WIDTH // 2), 1.0, 2.0).astype(np.float32)[None, :]

    def rows(real, imag):
        both = np.stack([real.T, imag.T]).reshape(2, 4, CHUNKS, JB, WIDTH)
        return both.transpose(1, 2, 0, 3, 4).reshape(2 * KP, WIDTH).astype(BF16)

    return rows(cosine, -sine), rows(cosine * weight, -sine * weight)


def lat_tables():
    pos = np.arange(LAT)
    angle = (pos[:, None] * pos[None, :] % LAT).astype(np.float32) * np.float32(2.0 * math.pi / LAT)
    factor = np.float32(1.0 / math.sqrt(LAT))
    cosine = np.cos(angle) * factor

    def real_form(sign):
        sine = np.sin(angle) * np.float32(factor * sign)
        return np.stack([np.stack([cosine, -sine], -1), np.stack([sine, cosine], -1)], 1).astype(BF16)

    fwd = real_form(-1.0).transpose(1, 0, 3, 2).reshape(2 * LAT, 2 * LAT)
    inv = real_form(1.0).transpose(3, 2, 1, 0).reshape(2 * LAT, 2 * LAT)
    return fwd, inv, np.ascontiguousarray(fwd.T)


def dot(a, b):
    return jnp.dot(a, b, preferred_element_type=F32)


def dot_tb(a, b):
    return lax.dot_general(a, b, (((1,), (1,)), ((), ())), preferred_element_type=F32)


def dot_ta(a, b):
    return lax.dot_general(a, b, (((0,), (0,)), ((), ())), preferred_element_type=F32)


def kernel(
    field, cot, w1, b1, w2, b2, tf, ti, tt, l1, l2, l3,
    out, gw1, gb1, gw2, gb2,
    slab, send, recv, gsend, grecv, mixed, hidden, slope, mask, dsec, dfir, scr, bmat, wm, wtmp, bias, acc, gb,
    wraw, braw, packed, parts, shares, pieces, done, every,
    slab_sem, out_sem, par_sem, ssem, rsem, own_sem, rs_s, rs_r, sum_s, sum_r, all_s, all_r, ag_s, ag_r,
):
    batch, me = lax.axis_index("batch"), lax.axis_index("lat")
    half, zz, core = me // 8, (me // 2) % 4, me % 2

    def partner(o):
        dx, dz, dc = o
        return (half + dx) % 2, (zz + dz) % 4, (core + dc) % 2

    def index(part):
        return part[0] * 8 + part[1] * 2 + part[2]

    def source(o):
        dx, dz, dc = o
        return ((half + dx) % 2) * 8 + ((zz + 4 - dz) % 4) * 2 + (core + dc) % 2

    def slab_copy(ref, s, h):
        return pltpu.make_async_copy(ref.at[s, h], slab.at[s * LOCAL + h], slab_sem.at[s * LOCAL + h])

    for s in range(SAMPLES):
        for h in range(LOCAL):
            slab_copy(field, s, h).start()
    params = [
        pltpu.make_async_copy(w1.at[:, pl.ds(half * 4, 4)], wraw.at[0], par_sem.at[0]),
        pltpu.make_async_copy(w2.at[:, pl.ds(half * 4, 4)], wraw.at[1], par_sem.at[1]),
        pltpu.make_async_copy(b1, braw.at[0], par_sem.at[2]),
        pltpu.make_async_copy(b2, braw.at[1], par_sem.at[3]),
    ]
    for copy in params:
        copy.start()

    barrier = pltpu.get_barrier_semaphore()
    for o in OFFSETS:
        if o != (0, 0, 0):
            pl.semaphore_signal(barrier, inc=1, device_id=(batch, index(partner(o))), device_id_type=MESH)
    for o in range(1, BATCH):
        pl.semaphore_signal(barrier, inc=1, device_id=((batch + o) % BATCH, me), device_id_type=MESH)

    def lanes(part):
        return pl.ds(pl.multiple_of(part * HALF, 128), HALF)

    def rows16(quarter, jc):
        return pl.ds(pl.multiple_of(quarter * 48 + jc * 16, 16), 16)

    def chunk(jc):
        return pl.ds(pl.multiple_of(jc * 16, 16), 16)

    def inward(a, jc, i):
        to = partner(OFFSETS[i])
        src = send.at[a, to[2], :, rows16(to[1], jc), lanes(to[0])]
        dst = recv.at[a, me, :, chunk(jc), :]
        if OFFSETS[i] == (0, 0, 0):
            return pltpu.make_async_copy(src, dst, own_sem.at[a, jc])
        return pltpu.make_async_remote_copy(
            src, dst, ssem.at[a, jc, i], rsem.at[a, jc, i], device_id=(batch, index(to)), device_id_type=MESH
        )

    def inward_wait(a, jc, i):
        if OFFSETS[i] == (0, 0, 0):
            inward(a, jc, i).wait()
            return
        dst = recv.at[a, source(OFFSETS[i]), :, chunk(jc), :]
        pltpu.make_async_remote_copy(
            dst, dst, ssem.at[a, jc, i], rsem.at[a, jc, i], device_id=(batch, me), device_id_type=MESH
        ).wait_recv()

    def outward(jc, i):
        to = index(partner(OFFSETS[i]))
        src = gsend.at[pl.ds(to * LOCAL, LOCAL), chunk(jc), :]
        dst = grecv.at[core, :, rows16(zz, jc), lanes(half)]
        if OFFSETS[i] == (0, 0, 0):
            return pltpu.make_async_copy(src, dst, own_sem.at[2, jc])
        return pltpu.make_async_remote_copy(
            src, dst, ssem.at[2, jc, i], rsem.at[2, jc, i], device_id=(batch, to), device_id_type=MESH
        )

    def outward_wait(jc, i):
        if OFFSETS[i] == (0, 0, 0):
            outward(jc, i).wait()
            return
        dx, dz, dc = OFFSETS[i]
        fx, fz, fc = (half + dx) % 2, (zz + 4 - dz) % 4, (core + dc) % 2
        dst = grecv.at[fc, :, rows16(fz, jc), lanes(fx)]
        pltpu.make_async_remote_copy(
            dst, dst, ssem.at[2, jc, i], rsem.at[2, jc, i], device_id=(batch, me), device_id_type=MESH
        ).wait_recv()

    def longitude(a, s):
        table = (tf, ti)[a]
        ref = (field, cot)[a]

        def one(h, carry):
            slab_copy(ref, s, h).wait()
            send[a, s, h] = dot(table[...], slab[s * LOCAL + h]).astype(BF16)
            if a == 0:
                slab_copy(cot, s, h).start()
            return carry

        lax.fori_loop(0, LOCAL, one, 0)

    def to_sample(a, jc, s):
        for i, o in enumerate(OFFSETS):

            @pl.when((core + o[2]) % 2 == s)
            def _(i=i):
                inward(a, jc, i).start()

    longitude(0, 0)
    pl.semaphore_wait(barrier, len(OFFSETS) - 1 + BATCH - 1)
    to_sample(0, 0, 0)
    longitude(0, 1)
    to_sample(0, 0, 1)
    for jc in range(1, CHUNKS):
        for i in range(len(OFFSETS)):
            inward(0, jc, i).start()
    longitude(1, 0)
    longitude(1, 1)
    for jc in range(CHUNKS):
        for i in range(len(OFFSETS)):
            inward(1, jc, i).start()

    for copy in params:
        copy.wait()
    row_id = lax.broadcasted_iota(jnp.int32, (BS, HALF), 0)
    col_id = lax.broadcasted_iota(jnp.int32, (BS, HALF), 1)
    for w in range(2):
        for part in range(2):
            total = jnp.zeros((8, HALF), F32)
            for n in range(4):
                place = jnp.where(row_id + n * BS == col_id, 1.0, 0.0).astype(F32)
                placed = dot(wraw[w, part, n].astype(BF16), place.astype(BF16))
                wtmp[part, n * BS : (n + 1) * BS, :] = placed.astype(BF16)
                line = jnp.broadcast_to(braw[w, part, pl.ds(half * 4 + n, 1), :], (8, BS))
                total = total + jnp.dot(line, place, precision=lax.Precision.HIGHEST, preferred_element_type=F32)
            for t in range(TILES):
                c = (2 * t + part) * 128
                bias[w, :, c : c + 128] = total[:, t * 128 : (t + 1) * 128]
        for t in range(TILES):
            for u in range(TILES):
                real = wtmp[0, t * 128 : (t + 1) * 128, u * 128 : (u + 1) * 128]
                imag = wtmp[1, t * 128 : (t + 1) * 128, u * 128 : (u + 1) * 128]
                r, c = t * 256, u * 256
                wm[w, r : r + 128, c : c + 128] = real
                wm[w, r : r + 128, c + 128 : c + 256] = imag
                wm[w, r + 128 : r + 256, c : c + 128] = -imag
                wm[w, r + 128 : r + 256, c + 128 : c + 256] = real
    acc[...] = jnp.zeros_like(acc)
    gb[...] = jnp.zeros_like(gb)

    def gather(a, jc):
        for i in range(len(OFFSETS)):
            inward_wait(a, jc, i)

        def one(l, carry):
            rows = recv[a, l, :, chunk(jc), :].astype(F32).reshape(LOCAL * 16, HALF)
            for t in range(TILES):
                scr[t, pl.ds(pl.multiple_of(l * 96, 8), 96), :] = rows[:, t * 128 : (t + 1) * 128]
            return carry

        lax.fori_loop(0, 16, one, 0)

    def column(j):
        parts = [
            jnp.concatenate([scr[t, pl.ds(q * JB + j, LAT, stride=16), :] for t in range(TILES)], axis=1)
            for q in range(2)
        ]
        return jnp.concatenate(parts, axis=0).astype(BF16)

    def row_block(jc, rb):
        return pl.ds(pl.multiple_of(jc * ROWS + rb * RB, 128), RB)

    def forward(jc, carry):
        gather(0, jc)

        def one(j, c):
            res = dot(l1[...], column(j))
            rows = pl.ds(pl.multiple_of(jc * ROWS + j * LAT, 32), LAT)
            for p in range(2):
                for t in range(TILES):
                    mixed[rows, (2 * t + p) * 128 : (2 * t + p + 1) * 128] = res[
                        p * LAT : (p + 1) * LAT, t * 128 : (t + 1) * 128
                    ].astype(BF16)
            return c

        lax.fori_loop(0, JB, one, 0)

        def mix(rb, c):
            rows = row_block(jc, rb)
            for t in range(TILES):
                lo, hi = WIN[t]
                cols = slice(t * 256, (t + 1) * 256)
                x = dot(mixed[rows, lo:hi], wm[0, lo:hi, cols]) + bias[0, 0:1, cols]
                c0, c1 = math.sqrt(2.0 / math.pi), 0.044715
                xx = x * x
                th = jnp.tanh(x * (c0 + (c0 * c1) * xx))
                gate = 0.5 + 0.5 * th
                hidden[rows, cols] = (x * gate).astype(BF16)
                rise = (0.5 * x) * (1.0 - th * th) * (c0 + (3.0 * c0 * c1) * xx)
                slope[rows, cols] = (gate + rise).astype(BF16)
            for t in range(TILES):
                lo, hi = WIN[t]
                cols = slice(t * 256, (t + 1) * 256)
                y = dot(hidden[rows, lo:hi], wm[1, lo:hi, cols]) + bias[1, 0:1, cols]
                th = jnp.tanh(4.0 * y)
                mask[rows, cols] = (th * th).astype(BF16)
            return c

        lax.fori_loop(0, 2, mix, 0)
        return carry

    lax.fori_loop(0, CHUNKS, forward, 0)

    def backward(jc, carry):
        gather(1, jc)

        def one(j, c):
            res = dot(l2[...], column(j)).astype(BF16)
            rows = pl.ds(pl.multiple_of(jc * ROWS + j * LAT, 32), LAT)
            here = pl.ds(pl.multiple_of(j * LAT, 32), LAT)
            for p in range(2):
                for t in range(TILES):
                    cols = slice((2 * t + p) * 128, (2 * t + p + 1) * 128)
                    part = res[p * LAT : (p + 1) * LAT, t * 128 : (t + 1) * 128].astype(F32)
                    dsec[here, cols] = (part * mask[rows, cols].astype(F32)).astype(BF16)
            return c

        lax.fori_loop(0, JB, one, 0)

        def mix(rb, c):
            rows = row_block(jc, rb)
            here = pl.ds(pl.multiple_of(rb * RB, 128), RB)
            for t in range(TILES):
                lo, hi = WIN[t]
                cols = slice(t * 256, (t + 1) * 256)
                d = dot_tb(dsec[here, lo:hi], wm[1, cols, lo:hi])
                dfir[here, cols] = (d * slope[rows, cols].astype(F32)).astype(BF16)
            for t in range(TILES):
                lo, hi = WIN[t]
                cols = slice(t * 256, (t + 1) * 256)
                d = dot_tb(dfir[here, lo:hi], wm[0, cols, lo:hi]).astype(BF16)
                for jl in range(JB // 2):
                    for p in range(2):
                        bmat[rb * (JB // 2) + jl, p * LAT : (p + 1) * LAT, t * 128 : (t + 1) * 128] = d[
                            jl * LAT : (jl + 1) * LAT, p * 128 : (p + 1) * 128
                        ]
            return c

        lax.fori_loop(0, 2, mix, 0)

        def last(j, c):
            res = dot(l3[...], bmat[j])
            for q in range(2):
                for t in range(TILES):
                    scr[t, pl.ds(q * JB + j, LAT, stride=16), :] = res[
                        q * LAT : (q + 1) * LAT, t * 128 : (t + 1) * 128
                    ]
            return c

        lax.fori_loop(0, JB, last, 0)

        def pack(l, c):
            for t in range(TILES):
                part = scr[t, pl.ds(pl.multiple_of(l * 96, 8), 96), :]
                gsend[pl.ds(l * LOCAL, LOCAL), chunk(jc), t * 128 : (t + 1) * 128] = part.astype(BF16).reshape(
                    LOCAL, 16, 128
                )
            return c

        lax.fori_loop(0, 16, pack, 0)
        for i in range(len(OFFSETS)):
            outward(jc, i).start()

        here = pl.ds(pl.multiple_of(jc * ROWS, 128), ROWS)
        for t in range(TILES):
            lo, hi = WIN[t]
            cols = slice(t * 256, (t + 1) * 256)
            acc[1, cols, lo:hi] += dot_ta(hidden[here, cols], dsec[:, lo:hi])
            acc[0, cols, lo:hi] += dot_ta(mixed[here, cols], dfir[:, lo:hi])
        ones = jnp.ones((16, ROWS), BF16)
        gb[0] += dot(ones, dfir[...])[0:8]
        gb[1] += dot(ones, dsec[...])[0:8]
        return carry

    lax.fori_loop(0, CHUNKS, backward, 0)

    lane = lax.broadcasted_iota(jnp.int32, (BS, 128), 1)
    for w in range(2):
        for part in range(2):
            for t in range(TILES):

                def block(n):
                    found = []
                    for u, lo, hi in PIECES[n]:
                        r, c = u * 256, t * 256
                        top = acc[w, r + lo : r + hi, c + part * 128 : c + (part + 1) * 128]
                        low = acc[w, r + 128 + lo : r + 128 + hi, c + (1 - part) * 128 : c + (2 - part) * 128]
                        found.append(top + low if part == 0 else top - low)
                    return found[0] if len(found) == 1 else jnp.concatenate(found, axis=0)

                tile = jnp.where(lane < 96 - 32 * t, block(t), block(t + 1)).astype(BF16)
                for i in range(3):
                    u = ((w * 2 + part) * TILES + t) * 3 + i
                    packed[u // UNITS, u % UNITS] = tile[i * 32 : (i + 1) * 32]
    row = lax.broadcasted_iota(jnp.int32, (32, 128), 0)
    lines = jnp.zeros((32, 128), F32)
    for w in range(2):
        for part in range(2):
            for t in range(TILES):
                line = gb[w, 0:1, (2 * t + part) * 128 : (2 * t + part + 1) * 128]
                lines = jnp.where(row == (w * 2 + part) * TILES + t, jnp.broadcast_to(line, (32, 128)), lines)
    packed[7, 1] = lines.astype(BF16)
    for u in range(2, UNITS):
        packed[7, u] = jnp.zeros((32, 128), BF16)

    def share(o):
        to = (batch + o) % BATCH
        return pltpu.make_async_remote_copy(
            packed.at[to], parts.at[batch], rs_s.at[o], rs_r.at[o], device_id=(to, me), device_id_type=MESH
        )

    def share_wait(o):
        dst = parts.at[(batch + BATCH - o) % BATCH]
        pltpu.make_async_remote_copy(
            dst, dst, rs_s.at[o], rs_r.at[o], device_id=(batch, me), device_id_type=MESH
        ).wait_recv()

    for o in range(1, BATCH):
        share(o).start()
    parts[batch] = packed[batch]
    for o in range(1, BATCH):
        share_wait(o)
    total = parts[0].astype(F32)
    for o in range(1, BATCH):
        total = total + parts[o].astype(F32)
    shares[...] = total

    mine = me % 8

    def to_reducer(g):
        return pltpu.make_async_remote_copy(
            shares.at[g], pieces.at[mine], sum_s.at[g], sum_r.at[mine],
            device_id=(batch, half * 8 + g), device_id_type=MESH,
        )

    def to_all(i):
        return pltpu.make_async_remote_copy(
            done.at[half, mine], done.at[half, mine], all_s.at[i], all_r.at[half, mine],
            device_id=(batch, index(partner(OFFSETS[i]))), device_id_type=MESH,
        )

    for g in range(UNITS):

        @pl.when(mine != g)
        def _(g=g):
            to_reducer(g).start()

    @pl.when(mine < UNITS)
    def _():
        pieces[mine] = shares[mine]
        for g in range(8):

            @pl.when(mine != g)
            def _(g=g):
                dst = pieces.at[g]
                pltpu.make_async_remote_copy(
                    dst, dst, sum_s.at[0], sum_r.at[g], device_id=(batch, me), device_id_type=MESH
                ).wait_recv()

        whole = pieces[0]
        for g in range(1, 8):
            whole = whole + pieces[g]
        samples = SAMPLES * BATCH
        done[half, mine] = (whole * (1.0 / math.sqrt(samples * LAT * (WIDTH // 2 + 1)))).astype(BF16)
        for i, o in enumerate(OFFSETS):
            if o != (0, 0, 0):
                to_all(i).start()

    for hf in range(2):
        for g in range(UNITS):

            @pl.when(me != hf * 8 + g)
            def _(hf=hf, g=g):
                dst = done.at[hf, g]
                pltpu.make_async_remote_copy(
                    dst, dst, all_s.at[0], all_r.at[hf, g], device_id=(batch, me), device_id_type=MESH
                ).wait_recv()

    def gathered(o):
        to = (batch + o) % BATCH
        return pltpu.make_async_remote_copy(
            done, every.at[batch], ag_s.at[o], ag_r.at[o], device_id=(to, me), device_id_type=MESH
        )

    for o in range(1, BATCH):
        gathered(o).start()
    every[batch] = done[...]

    for jc in range(CHUNKS):
        for i in range(len(OFFSETS)):
            outward_wait(jc, i)

    def final(h, carry):
        for s in range(SAMPLES):
            slab[s * LOCAL + h] = dot(tt[...], grecv[s, h]).astype(BF16)
            pltpu.make_async_copy(slab.at[s * LOCAL + h], out.at[s, h], out_sem.at[s * LOCAL + h]).start()
        return carry

    lax.fori_loop(0, LOCAL, final, 0)

    for o in range(1, BATCH):
        dst = every.at[(batch + BATCH - o) % BATCH]
        pltpu.make_async_remote_copy(
            dst, dst, ag_s.at[o], ag_r.at[o], device_id=(batch, me), device_id_type=MESH
        ).wait_recv()
    for w, gw, gbias in ((0, gw1, gb1), (1, gw2, gb2)):
        for part in range(2):
            for hf in range(2):
                tiles, lines = [], []
                for t in range(TILES):
                    k = (w * 2 + part) * TILES + t
                    found = [every[u // UNITS, hf, u % UNITS] for u in range(3 * k, 3 * k + 3)]
                    tiles.append(jnp.concatenate(found, axis=0).astype(F32))
                    lines.append(jnp.broadcast_to(every[7, hf, 1].astype(F32)[k : k + 1], (8, 128)))

                def blocks(x, n):
                    if n == 0:
                        return x[0][:, :BS]
                    if n == 3:
                        return pltpu.roll(x[2], BS, 1)[:, :BS]
                    return pltpu.roll(jnp.concatenate(x[n - 1 : n + 1], axis=1), 128 + 32 * n, 1)[:, :BS]

                for n in range(4):
                    gw[part, hf * 4 + n] = blocks(tiles, n)
                    gbias[part, hf * 4 + n : hf * 4 + n + 1, :] = blocks(lines, n)[0:1]

    for o in range(1, BATCH):
        share(o).wait_send()
        gathered(o).wait_send()
    for g in range(UNITS):

        @pl.when(mine != g)
        def _(g=g):
            to_reducer(g).wait_send()

    @pl.when(mine < UNITS)
    def _():
        for i, o in enumerate(OFFSETS):
            if o != (0, 0, 0):
                to_all(i).wait_send()

    for a in range(3):
        for jc in range(CHUNKS):
            for i, o in enumerate(OFFSETS):
                if o != (0, 0, 0):
                    (outward(jc, i) if a == 2 else inward(a, jc, i)).wait_send()
    for s in range(SAMPLES):
        for h in range(LOCAL):
            pltpu.make_async_copy(slab.at[s * LOCAL + h], out.at[s, h], out_sem.at[s * LOCAL + h]).wait()


def local(field, cotangent, weight_one, bias_one, weight_two, bias_two):
    tf, ti = lon_tables()
    tt = np.ascontiguousarray(tf.T)
    l1, l2, l3 = lat_tables()
    hbm, vmem = pl.BlockSpec(memory_space=pl.ANY), pl.BlockSpec(memory_space=pltpu.VMEM)
    n_off = len(OFFSETS)
    return pl.pallas_call(
        kernel,
        name="afno_backward",
        out_shape=(
            jax.ShapeDtypeStruct(field.shape, BF16),
            jax.ShapeDtypeStruct(weight_one.shape, F32),
            jax.ShapeDtypeStruct(bias_one.shape, F32),
            jax.ShapeDtypeStruct(weight_two.shape, F32),
            jax.ShapeDtypeStruct(bias_two.shape, F32),
        ),
        in_specs=[hbm] * 6 + [vmem] * 6,
        out_specs=(hbm, vmem, vmem, vmem, vmem),
        scratch_shapes=[
            pltpu.VMEM((SAMPLES * LOCAL, WIDTH, CH), BF16),
            pltpu.VMEM((2, SAMPLES, LOCAL, 2 * KP, CH), BF16),
            pltpu.VMEM((2, 16, LOCAL, 2 * QUARTER, HALF), BF16),
            pltpu.VMEM((LAT, 2 * QUARTER, HALF), BF16),
            pltpu.VMEM((SAMPLES, LOCAL, 2 * KP, CH), BF16),
            pltpu.VMEM((CHUNKS * ROWS, CH), BF16),
            pltpu.VMEM((CHUNKS * ROWS, CH), BF16),
            pltpu.VMEM((CHUNKS * ROWS, CH), BF16),
            pltpu.VMEM((CHUNKS * ROWS, CH), BF16),
            pltpu.VMEM((ROWS, CH), BF16),
            pltpu.VMEM((ROWS, CH), BF16),
            pltpu.VMEM((TILES, LAT * 16, 128), F32),
            pltpu.VMEM((JB, 2 * LAT, HALF), BF16),
            pltpu.VMEM((2, CH, CH), BF16),
            pltpu.VMEM((2, HALF, HALF), BF16),
            pltpu.VMEM((2, 8, CH), F32),
            pltpu.VMEM((2, CH, CH), F32),
            pltpu.VMEM((2, 8, CH), F32),
            pltpu.VMEM((2, 2, 4, BS, BS), F32),
            pltpu.VMEM((2, 2, 8, BS), F32),
            pltpu.VMEM((BATCH, UNITS, 32, 128), BF16),
            pltpu.VMEM((BATCH, UNITS, 32, 128), BF16),
            pltpu.VMEM((UNITS, 32, 128), F32),
            pltpu.VMEM((8, 32, 128), F32),
            pltpu.VMEM((2, UNITS, 32, 128), BF16),
            pltpu.VMEM((BATCH, 2, UNITS, 32, 128), BF16),
            pltpu.SemaphoreType.DMA((SAMPLES * LOCAL,)),
            pltpu.SemaphoreType.DMA((SAMPLES * LOCAL,)),
            pltpu.SemaphoreType.DMA((4,)),
            pltpu.SemaphoreType.DMA((3, CHUNKS, n_off)),
            pltpu.SemaphoreType.DMA((3, CHUNKS, n_off)),
            pltpu.SemaphoreType.DMA((3, CHUNKS)),
            pltpu.SemaphoreType.DMA((BATCH,)),
            pltpu.SemaphoreType.DMA((BATCH,)),
            pltpu.SemaphoreType.DMA((UNITS,)),
            pltpu.SemaphoreType.DMA((8,)),
            pltpu.SemaphoreType.DMA((n_off,)),
            pltpu.SemaphoreType.DMA((2, UNITS)),
            pltpu.SemaphoreType.DMA((BATCH,)),
            pltpu.SemaphoreType.DMA((BATCH,)),
        ],
        compiler_params=pltpu.CompilerParams(
            collective_id=0, has_side_effects=True, vmem_limit_bytes=62 * 1024 * 1024
        ),
        cost_estimate=pl.CostEstimate(flops=10**10, bytes_accessed=10**7, transcendentals=4 * 10**6),
    )(field, cotangent, weight_one, bias_one, weight_two, bias_two, tf, ti, tt, l1, l2, l3)


def solution(mesh):
    in_specs = (P("batch", "lat", None, None), P("batch", "lat", None, None), P(), P(), P(), P())
    out_specs = (P("batch", "lat", None, None), P(), P(), P(), P())
    return jax.shard_map(local, mesh=mesh, in_specs=in_specs, out_specs=out_specs, check_vma=False)
```

```python
import functools
import math

import jax
import jax.numpy as jnp
import numpy as np
from jax import lax
from jax.experimental import pallas as pl
from jax.experimental.pallas import tpu as pltpu
from jax.sharding import PartitionSpec as P

MESH = pl.DeviceIdType.MESH
F32, BF16 = jnp.float32, jnp.bfloat16
NY = 4
BATCH = 2 * NY
UNITS = 5
KP = 96
QUARTER = 24
JB = 8
CHUNKS = QUARTER // JB
HALF = 384
TILES = HALF // 128
LOCAL = 6
SAMPLES = 2
LAT = 96
WIDTH = 180
CH = 768
BS = 96
ROWS = JB * LAT
RB = ROWS // 2
OFFSETS = [(dx, dz, dc) for dz in (1, 3, 2, 0) for dx in (1, 0) for dc in (1, 0)]
CUTS = (10, 20, 26)
WIN = [(0, 512), (0, 768), (256, 768)]
PIECES = [[(0, 0, 96)], [(0, 96, 128), (1, 0, 64)], [(1, 64, 128), (2, 0, 32)], [(2, 32, 128)]]


def lon_tables():
    wpos, kpos = np.arange(WIDTH), np.arange(KP)
    angle = (wpos[:, None] * kpos[None, :] % WIDTH).astype(np.float32) * np.float32(2.0 * math.pi / WIDTH)
    valid = (kpos <= WIDTH // 2).astype(np.float32)[None, :]
    factor = np.float32(1.0 / math.sqrt(WIDTH))
    cosine, sine = np.cos(angle) * valid * factor, np.sin(angle) * valid * factor
    weight = np.where((kpos == 0) | (kpos == WIDTH // 2), 1.0, 2.0).astype(np.float32)[None, :]

    def rows(real, imag):
        both = np.stack([real.T, imag.T]).reshape(2, 4, CHUNKS, JB, WIDTH)
        return both.transpose(1, 2, 0, 3, 4).reshape(2 * KP, WIDTH).astype(BF16)

    def paired(table):
        both = np.zeros((SAMPLES, 2 * KP, WIDTH, SAMPLES), BF16)
        for s in range(SAMPLES):
            both[s, :, :, s] = table
        return both.reshape(SAMPLES * 2 * KP, WIDTH * SAMPLES)

    return paired(rows(cosine, -sine)), paired(rows(cosine * weight, -sine * weight))


def lat_tables():
    pos = np.arange(LAT)
    angle = (pos[:, None] * pos[None, :] % LAT).astype(np.float32) * np.float32(2.0 * math.pi / LAT)
    factor = np.float32(1.0 / math.sqrt(LAT))
    cosine = np.cos(angle) * factor

    def real_form(sign):
        sine = np.sin(angle) * np.float32(factor * sign)
        return np.stack([np.stack([cosine, -sine], -1), np.stack([sine, cosine], -1)], 1).astype(BF16)

    fwd = real_form(-1.0).transpose(1, 0, 3, 2).reshape(2 * LAT, 2 * LAT)
    inv = real_form(1.0).transpose(3, 2, 1, 0).reshape(2 * LAT, 2 * LAT)
    return fwd, inv, np.ascontiguousarray(fwd.T)


def dot(a, b):
    return jnp.dot(a, b, preferred_element_type=F32)


def dot_tb(a, b):
    return lax.dot_general(a, b, (((1,), (1,)), ((), ())), preferred_element_type=F32)


def dot_ta(a, b):
    return lax.dot_general(a, b, (((0,), (0,)), ((), ())), preferred_element_type=F32)


def kernel(
    field, cot, w1, b1, w2, b2, tf_hbm, ti_hbm, l1_hbm, l2_hbm, l3_hbm,
    grecv, every,
    slab, send, recv, gsend, mixed, hidden, slope, mask, dsec, dfir, scr, bmat, wm, wtmp, bias, acc, gb,
    wraw, braw, packed, parts, shares, pieces, done, tf, ti, l1, l2, l3,
    table_sem, slab_sem, every_sem, par_sem, ssem, rsem, own_sem, rs_s, rs_r, sum_s, sum_r, all_s, all_r, ag_s, ag_r,
):
    batch, me = lax.axis_index("batch"), lax.axis_index("lat")
    half, zz, core = me // 8, (me // 2) % 4, me % 2
    side, yy = batch // NY, batch % NY
    other = (1 - side) * NY + yy

    def along(o):
        return side * NY + (yy + o) % NY

    def partner(o):
        dx, dz, dc = o
        return (half + dx) % 2, (zz + dz) % 4, (core + dc) % 2

    def index(part):
        return part[0] * 8 + part[1] * 2 + part[2]

    def source(o):
        dx, dz, dc = o
        return ((half + dx) % 2) * 8 + ((zz + 4 - dz) % 4) * 2 + (core + dc) % 2

    def slab_copy(a, h):
        return pltpu.make_async_copy((field, cot)[a].at[h], slab.at[a, h], slab_sem.at[a, h])

    tables = [
        pltpu.make_async_copy(src, dst, table_sem.at[i])
        for i, (src, dst) in enumerate(((tf_hbm, tf), (ti_hbm, ti), (l1_hbm, l1), (l2_hbm, l2), (l3_hbm, l3)))
    ]
    tables[0].start()
    for h in range(LOCAL):
        slab_copy(0, h).start()
    for copy in tables[1:]:
        copy.start()
    params = [
        pltpu.make_async_copy(w1.at[:, pl.ds(half * 4, 4)], wraw.at[0], par_sem.at[0]),
        pltpu.make_async_copy(w2.at[:, pl.ds(half * 4, 4)], wraw.at[1], par_sem.at[1]),
        pltpu.make_async_copy(b1, braw.at[0], par_sem.at[2]),
        pltpu.make_async_copy(b2, braw.at[1], par_sem.at[3]),
    ]
    for copy in params:
        copy.start()

    barrier = pltpu.get_barrier_semaphore()
    for o in OFFSETS:
        if o != (0, 0, 0):
            pl.semaphore_signal(barrier, inc=1, device_id=(batch, index(partner(o))), device_id_type=MESH)
        pl.semaphore_signal(barrier, inc=1, device_id=(other, index(partner(o))), device_id_type=MESH)
    for o in range(1, NY):
        for to in (along(o), (1 - side) * NY + (yy + o) % NY):
            pl.semaphore_signal(barrier, inc=1, device_id=(to, me), device_id_type=MESH)

    def lanes(part):
        return pl.ds(pl.multiple_of(part * HALF, 128), HALF)

    def rows16(sample, quarter, jc):
        return pl.ds(pl.multiple_of(sample * 2 * KP + quarter * 48 + jc * 16, 16), 16)

    def chunk(jc):
        return pl.ds(pl.multiple_of(jc * 16, 16), 16)

    def inward(a, jc, i):
        to = partner(OFFSETS[i])
        src = send.at[a, :, rows16(to[2], to[1], jc), lanes(to[0])]
        dst = recv.at[a, me, :, chunk(jc), :]
        if OFFSETS[i] == (0, 0, 0):
            return pltpu.make_async_copy(src, dst, own_sem.at[a, jc])
        return pltpu.make_async_remote_copy(
            src, dst, ssem.at[a, jc, i], rsem.at[a, jc, i], device_id=(batch, index(to)), device_id_type=MESH
        )

    def inward_wait(a, jc, i):
        if OFFSETS[i] == (0, 0, 0):
            inward(a, jc, i).wait()
            return
        dst = recv.at[a, source(OFFSETS[i]), :, chunk(jc), :]
        pltpu.make_async_remote_copy(
            dst, dst, ssem.at[a, jc, i], rsem.at[a, jc, i], device_id=(batch, me), device_id_type=MESH
        ).wait_recv()

    def outward(jc, i):
        to = index(partner(OFFSETS[i]))
        src = gsend.at[pl.ds(to * LOCAL, LOCAL), chunk(jc), :]
        dst = grecv.at[:, rows16(core, zz, jc), lanes(half)]
        if OFFSETS[i] == (0, 0, 0):
            return pltpu.make_async_copy(src, dst, own_sem.at[2, jc])
        return pltpu.make_async_remote_copy(
            src, dst, ssem.at[2, jc, i], rsem.at[2, jc, i], device_id=(batch, to), device_id_type=MESH
        )

    def outward_wait(jc, i):
        if OFFSETS[i] == (0, 0, 0):
            outward(jc, i).wait()
            return
        dx, dz, dc = OFFSETS[i]
        fx, fz, fc = (half + dx) % 2, (zz + 4 - dz) % 4, (core + dc) % 2
        dst = grecv.at[:, rows16(fc, fz, jc), lanes(fx)]
        pltpu.make_async_remote_copy(
            dst, dst, ssem.at[2, jc, i], rsem.at[2, jc, i], device_id=(batch, me), device_id_type=MESH
        ).wait_recv()

    def longitude(a):
        table = (tf, ti)[a]

        def one(h, carry):
            slab_copy(a, h).wait()
            if a == 0:
                slab_copy(1, h).start()
            pair = slab[a, h].reshape(WIDTH * SAMPLES, CH)
            send[a, h] = dot(table[...], pair).astype(BF16)
            return carry

        lax.fori_loop(0, LOCAL, one, 0)

    tables[0].wait()
    longitude(0)
    pl.semaphore_wait(barrier, 2 * len(OFFSETS) - 1 + 2 * (NY - 1))
    for jc in range(CHUNKS):
        for i in range(len(OFFSETS)):
            inward(0, jc, i).start()
    tables[1].wait()
    longitude(1)
    for jc in range(CHUNKS):
        for i in range(len(OFFSETS)):
            inward(1, jc, i).start()

    for copy in params + tables[2:]:
        copy.wait()
    row_id = lax.broadcasted_iota(jnp.int32, (BS, HALF), 0)
    col_id = lax.broadcasted_iota(jnp.int32, (BS, HALF), 1)
    for w in range(2):
        for part in range(2):
            total = jnp.zeros((8, HALF), F32)
            for n in range(4):
                place = jnp.where(row_id + n * BS == col_id, 1.0, 0.0).astype(F32)
                placed = dot(wraw[w, part, n].astype(BF16), place.astype(BF16))
                wtmp[part, n * BS : (n + 1) * BS, :] = placed.astype(BF16)
                line = jnp.broadcast_to(braw[w, part, pl.ds(half * 4 + n, 1), :], (8, BS))
                total = total + jnp.dot(line, place, precision=lax.Precision.HIGHEST, preferred_element_type=F32)
            for t in range(TILES):
                c = (2 * t + part) * 128
                bias[w, :, c : c + 128] = total[:, t * 128 : (t + 1) * 128]
        for t in range(TILES):
            for u in range(TILES):
                real = wtmp[0, t * 128 : (t + 1) * 128, u * 128 : (u + 1) * 128]
                imag = wtmp[1, t * 128 : (t + 1) * 128, u * 128 : (u + 1) * 128]
                r, c = t * 256, u * 256
                wm[w, r : r + 128, c : c + 128] = real
                wm[w, r : r + 128, c + 128 : c + 256] = imag
                wm[w, r + 128 : r + 256, c : c + 128] = -imag
                wm[w, r + 128 : r + 256, c + 128 : c + 256] = real
    acc[...] = jnp.zeros_like(acc)
    gb[...] = jnp.zeros_like(gb)

    def gather(a, jc):
        for i in range(len(OFFSETS)):
            inward_wait(a, jc, i)

        def one(l, carry):
            rows = recv[a, l, :, chunk(jc), :].astype(F32).reshape(LOCAL * 16, HALF)
            for t in range(TILES):
                scr[t, pl.ds(pl.multiple_of(l * 96, 8), 96), :] = rows[:, t * 128 : (t + 1) * 128]
            return carry

        lax.fori_loop(0, 16, one, 0)

    def column(j):
        parts = [
            jnp.concatenate([scr[t, pl.ds(q * JB + j, LAT, stride=16), :] for t in range(TILES)], axis=1)
            for q in range(2)
        ]
        return jnp.concatenate(parts, axis=0).astype(BF16)

    def row_block(jc, rb):
        return pl.ds(pl.multiple_of(jc * ROWS + rb * RB, 128), RB)

    def forward(jc, carry):
        gather(0, jc)

        def one(j, c):
            res = dot(l1[...], column(j))
            rows = pl.ds(pl.multiple_of(jc * ROWS + j * LAT, 32), LAT)
            for p in range(2):
                for t in range(TILES):
                    mixed[rows, (2 * t + p) * 128 : (2 * t + p + 1) * 128] = res[
                        p * LAT : (p + 1) * LAT, t * 128 : (t + 1) * 128
                    ].astype(BF16)
            return c

        lax.fori_loop(0, JB, one, 0)

        def mix(rb, c):
            rows = row_block(jc, rb)
            for t in range(TILES):
                lo, hi = WIN[t]
                cols = slice(t * 256, (t + 1) * 256)
                x = dot(mixed[rows, lo:hi], wm[0, lo:hi, cols]) + bias[0, 0:1, cols]
                c0, c1 = math.sqrt(2.0 / math.pi), 0.044715
                xx = x * x
                th = jnp.tanh(x * (c0 + (c0 * c1) * xx))
                gate = 0.5 + 0.5 * th
                hidden[rows, cols] = (x * gate).astype(BF16)
                rise = (0.5 * x) * (1.0 - th * th) * (c0 + (3.0 * c0 * c1) * xx)
                slope[rows, cols] = (gate + rise).astype(BF16)
            for t in range(TILES):
                lo, hi = WIN[t]
                cols = slice(t * 256, (t + 1) * 256)
                y = dot(hidden[rows, lo:hi], wm[1, lo:hi, cols]) + bias[1, 0:1, cols]
                th = jnp.tanh(4.0 * y)
                mask[rows, cols] = (th * th).astype(BF16)
            return c

        lax.fori_loop(0, 2, mix, 0)
        return carry

    lax.fori_loop(0, CHUNKS, forward, 0)

    def backward(jc, carry):
        gather(1, jc)

        def one(j, c):
            res = dot(l2[...], column(j)).astype(BF16)
            rows = pl.ds(pl.multiple_of(jc * ROWS + j * LAT, 32), LAT)
            here = pl.ds(pl.multiple_of(j * LAT, 32), LAT)
            for p in range(2):
                for t in range(TILES):
                    cols = slice((2 * t + p) * 128, (2 * t + p + 1) * 128)
                    part = res[p * LAT : (p + 1) * LAT, t * 128 : (t + 1) * 128].astype(F32)
                    dsec[here, cols] = (part * mask[rows, cols].astype(F32)).astype(BF16)
            return c

        lax.fori_loop(0, JB, one, 0)

        def mix(rb, c):
            rows = row_block(jc, rb)
            here = pl.ds(pl.multiple_of(rb * RB, 128), RB)
            for t in range(TILES):
                lo, hi = WIN[t]
                cols = slice(t * 256, (t + 1) * 256)
                d = dot_tb(dsec[here, lo:hi], wm[1, cols, lo:hi])
                dfir[here, cols] = (d * slope[rows, cols].astype(F32)).astype(BF16)
            for t in range(TILES):
                lo, hi = WIN[t]
                cols = slice(t * 256, (t + 1) * 256)
                d = dot_tb(dfir[here, lo:hi], wm[0, cols, lo:hi]).astype(BF16)
                for jl in range(JB // 2):
                    for p in range(2):
                        bmat[rb * (JB // 2) + jl, p * LAT : (p + 1) * LAT, t * 128 : (t + 1) * 128] = d[
                            jl * LAT : (jl + 1) * LAT, p * 128 : (p + 1) * 128
                        ]
            return c

        lax.fori_loop(0, 2, mix, 0)

        def last(j, c):
            res = dot(l3[...], bmat[j])
            for q in range(2):
                for t in range(TILES):
                    scr[t, pl.ds(q * JB + j, LAT, stride=16), :] = res[
                        q * LAT : (q + 1) * LAT, t * 128 : (t + 1) * 128
                    ]
            return c

        lax.fori_loop(0, JB, last, 0)

        def pack(l, c):
            for t in range(TILES):
                part = scr[t, pl.ds(pl.multiple_of(l * 96, 8), 96), :]
                gsend[pl.ds(l * LOCAL, LOCAL), chunk(jc), t * 128 : (t + 1) * 128] = part.astype(BF16).reshape(
                    LOCAL, 16, 128
                )
            return c

        lax.fori_loop(0, 16, pack, 0)

        @pl.when(jc < 1)
        def _():
            for i in range(len(OFFSETS)):
                outward(jc, i).start()

        here = pl.ds(pl.multiple_of(jc * ROWS, 128), ROWS)
        for t in range(TILES):
            lo, hi = WIN[t]
            cols = slice(t * 256, (t + 1) * 256)
            acc[1, cols, lo:hi] += dot_ta(hidden[here, cols], dsec[:, lo:hi])
            acc[0, cols, lo:hi] += dot_ta(mixed[here, cols], dfir[:, lo:hi])
        ones = jnp.ones((16, ROWS), BF16)
        gb[0] += dot(ones, dfir[...])[0:8]
        gb[1] += dot(ones, dsec[...])[0:8]
        return carry

    lax.fori_loop(0, CHUNKS, backward, 0)

    lane = lax.broadcasted_iota(jnp.int32, (BS, 128), 1)
    for w in range(2):
        for part in range(2):
            for t in range(TILES):

                def block(n):
                    found = []
                    for u, lo, hi in PIECES[n]:
                        r, c = u * 256, t * 256
                        top = acc[w, r + lo : r + hi, c + part * 128 : c + (part + 1) * 128]
                        low = acc[w, r + 128 + lo : r + 128 + hi, c + (1 - part) * 128 : c + (2 - part) * 128]
                        found.append(top + low if part == 0 else top - low)
                    return found[0] if len(found) == 1 else jnp.concatenate(found, axis=0)

                tile = jnp.where(lane < 96 - 32 * t, block(t), block(t + 1)).astype(BF16)
                for i in range(3):
                    u = ((w * 2 + part) * TILES + t) * 3 + i
                    packed[u // UNITS, u % UNITS] = tile[i * 32 : (i + 1) * 32]
    row = lax.broadcasted_iota(jnp.int32, (32, 128), 0)
    lines = jnp.zeros((32, 128), F32)
    for w in range(2):
        for part in range(2):
            for t in range(TILES):
                line = gb[w, 0:1, (2 * t + part) * 128 : (2 * t + part + 1) * 128]
                lines = jnp.where(row == (w * 2 + part) * TILES + t, jnp.broadcast_to(line, (32, 128)), lines)
    packed[7, 1] = lines.astype(BF16)
    for u in range(2, UNITS):
        packed[7, u] = jnp.zeros((32, 128), BF16)

    def share(o):
        return pltpu.make_async_remote_copy(
            packed.at[(batch + o) % BATCH], parts.at[batch], rs_s.at[o], rs_r.at[o],
            device_id=((batch + o) % BATCH, me), device_id_type=MESH,
        )

    for o in range(1, BATCH):
        share(o).start()
    back = [(jc, i) for jc in range(1, CHUNKS) for i in range(len(OFFSETS))]
    for jc, i in back[:CUTS[0]]:
        outward(jc, i).start()
    parts[batch] = packed[batch]
    for o in range(1, BATCH):
        dst = parts.at[(batch + BATCH - o) % BATCH]
        pltpu.make_async_remote_copy(
            dst, dst, rs_s.at[o], rs_r.at[o], device_id=(batch, me), device_id_type=MESH
        ).wait_recv()
    total = parts[0].astype(F32)
    for o in range(1, BATCH):
        total = total + parts[o].astype(F32)
    shares[...] = total.astype(BF16)

    mine = me % 8

    def to_reducer(g):
        return pltpu.make_async_remote_copy(
            shares.at[g], pieces.at[mine], sum_s.at[g], sum_r.at[mine],
            device_id=(batch, half * 8 + g), device_id_type=MESH,
        )

    def to_all(i, far):
        return pltpu.make_async_remote_copy(
            done.at[side, half, mine], done.at[side, half, mine], all_s.at[i, far], all_r.at[side, half, mine],
            device_id=((batch, other)[far], index(partner(OFFSETS[i]))), device_id_type=MESH,
        )

    listeners = [(i, far) for i, o in enumerate(OFFSETS) for far in range(2) if (o, far) != ((0, 0, 0), 0)]
    for g in range(UNITS):

        @pl.when(mine != g)
        def _(g=g):
            to_reducer(g).start()

    for jc, i in back[CUTS[0] : CUTS[1]]:
        outward(jc, i).start()

    @pl.when(mine < UNITS)
    def _():
        pieces[mine] = shares[mine]
        for g in range(8):

            @pl.when(mine != g)
            def _(g=g):
                dst = pieces.at[g]
                pltpu.make_async_remote_copy(
                    dst, dst, sum_s.at[0], sum_r.at[g], device_id=(batch, me), device_id_type=MESH
                ).wait_recv()

        whole = pieces[0].astype(F32)
        for g in range(1, 8):
            whole = whole + pieces[g].astype(F32)
        samples = SAMPLES * 2 * NY
        done[side, half, mine] = (whole * (1.0 / math.sqrt(samples * LAT * (WIDTH // 2 + 1)))).astype(BF16)
        for i, far in listeners:
            to_all(i, far).start()

    for jc, i in back[CUTS[1] : CUTS[2]]:
        outward(jc, i).start()

    for sd in range(2):
        for hf in range(2):
            for g in range(UNITS):

                @pl.when((side != sd) | (half != hf) | (mine != g))
                def _(sd=sd, hf=hf, g=g):
                    dst = done.at[sd, hf, g]
                    pltpu.make_async_remote_copy(
                        dst, dst, all_s.at[0, 0], all_r.at[sd, hf, g], device_id=(batch, me), device_id_type=MESH
                    ).wait_recv()

    def gathered(o):
        return pltpu.make_async_remote_copy(
            done, every.at[yy], ag_s.at[o], ag_r.at[o], device_id=(along(o), me), device_id_type=MESH
        )

    for o in range(1, NY):
        gathered(o).start()
    kept = pltpu.make_async_copy(done, every.at[yy], every_sem)
    kept.start()
    for jc, i in back[CUTS[2] :]:
        outward(jc, i).start()

    for jc in range(CHUNKS):
        for i in range(len(OFFSETS)):
            outward_wait(jc, i)
    for o in range(1, NY):
        dst = every.at[(yy + NY - o) % NY]
        pltpu.make_async_remote_copy(
            dst, dst, ag_s.at[o], ag_r.at[o], device_id=(batch, me), device_id_type=MESH
        ).wait_recv()
    kept.wait()

    for o in range(1, BATCH):
        share(o).wait_send()
    for o in range(1, NY):
        gathered(o).wait_send()
    for g in range(UNITS):

        @pl.when(mine != g)
        def _(g=g):
            to_reducer(g).wait_send()

    @pl.when(mine < UNITS)
    def _():
        for i, far in listeners:
            to_all(i, far).wait_send()

    for a in range(3):
        for jc in range(CHUNKS):
            for i, o in enumerate(OFFSETS):
                if o != (0, 0, 0):
                    (outward(jc, i) if a == 2 else inward(a, jc, i)).wait_send()


def finish(
    every, grecv, tt, out, gw1_hbm, gb1_hbm, gw2_hbm, gb2_hbm,
    slab, pair, sums, table, gw1, gb1, gw2, gb2, in_sem, out_sem, par_sem,
):
    fetch = [pltpu.make_async_copy(tt, table, par_sem.at[0]), pltpu.make_async_copy(every, sums, par_sem.at[1])]
    fetch[1].start()
    fetch[0].start()
    for h in range(LOCAL):
        pltpu.make_async_copy(grecv.at[h], slab.at[h], in_sem.at[h]).start()
    fetch[1].wait()
    for w, gw, gbias in ((0, gw1, gb1), (1, gw2, gb2)):
        for part in range(2):
            for hf in range(2):
                tiles, lines = [], []
                for t in range(TILES):
                    k = (w * 2 + part) * TILES + t
                    found = [sums[u // UNITS % NY, u // UNITS // NY, hf, u % UNITS] for u in range(3 * k, 3 * k + 3)]
                    tiles.append(jnp.concatenate(found, axis=0).astype(F32))
                    lines.append(jnp.broadcast_to(sums[3, 1, hf, 1].astype(F32)[k : k + 1], (8, 128)))

                def blocks(x, n):
                    if n == 0:
                        return x[0][:, :BS]
                    if n == 3:
                        return pltpu.roll(x[2], BS, 1)[:, :BS]
                    return pltpu.roll(jnp.concatenate(x[n - 1 : n + 1], axis=1), 128 + 32 * n, 1)[:, :BS]

                for n in range(4):
                    gw[part, hf * 4 + n] = blocks(tiles, n)
                    gbias[part, hf * 4 + n : hf * 4 + n + 1, :] = blocks(lines, n)[0:1]
    outs = [
        pltpu.make_async_copy(src, dst, par_sem.at[2 + i])
        for i, (src, dst) in enumerate(((gw1, gw1_hbm), (gb1, gb1_hbm), (gw2, gw2_hbm), (gb2, gb2_hbm)))
    ]
    for copy in outs:
        copy.start()
    fetch[0].wait()

    def one(h, carry):
        pltpu.make_async_copy(grecv.at[h], slab.at[h], in_sem.at[h]).wait()
        pair[h] = dot(table[...], slab[h]).astype(BF16).reshape(WIDTH, SAMPLES, CH)
        pltpu.make_async_copy(pair.at[h], out.at[h], out_sem.at[h]).start()
        return carry

    lax.fori_loop(0, LOCAL, one, 0)
    for copy in outs:
        copy.wait()
    for h in range(LOCAL):
        pltpu.make_async_copy(pair.at[h], out.at[h], out_sem.at[h]).wait()


def local(field, cotangent, weight_one, bias_one, weight_two, bias_two):
    tf, ti = lon_tables()
    tt = np.ascontiguousarray(tf.T)
    l1, l2, l3 = lat_tables()
    hbm = pl.BlockSpec(memory_space=pl.ANY)
    n_off = len(OFFSETS)

    def pairs(x):
        return x.transpose(1, 2, 0, 3)

    grecv, every = pl.pallas_call(
        kernel,
        name="afno_backward",
        out_shape=(
            jax.ShapeDtypeStruct((LOCAL, SAMPLES * 2 * KP, CH), BF16),
            jax.ShapeDtypeStruct((NY, 2, 2, UNITS, 32, 128), BF16),
        ),
        in_specs=[hbm] * 11,
        out_specs=(hbm, hbm),
        scratch_shapes=[
            pltpu.VMEM((2, LOCAL, WIDTH, SAMPLES, CH), BF16),
            pltpu.VMEM((2, LOCAL, SAMPLES * 2 * KP, CH), BF16),
            pltpu.VMEM((2, 16, LOCAL, 2 * QUARTER, HALF), BF16),
            pltpu.VMEM((LAT, 2 * QUARTER, HALF), BF16),
            pltpu.VMEM((CHUNKS * ROWS, CH), BF16),
            pltpu.VMEM((CHUNKS * ROWS, CH), BF16),
            pltpu.VMEM((CHUNKS * ROWS, CH), BF16),
            pltpu.VMEM((CHUNKS * ROWS, CH), BF16),
            pltpu.VMEM((ROWS, CH), BF16),
            pltpu.VMEM((ROWS, CH), BF16),
            pltpu.VMEM((TILES, LAT * 16, 128), F32),
            pltpu.VMEM((JB, 2 * LAT, HALF), BF16),
            pltpu.VMEM((2, CH, CH), BF16),
            pltpu.VMEM((2, HALF, HALF), BF16),
            pltpu.VMEM((2, 8, CH), F32),
            pltpu.VMEM((2, CH, CH), F32),
            pltpu.VMEM((2, 8, CH), F32),
            pltpu.VMEM((2, 2, 4, BS, BS), F32),
            pltpu.VMEM((2, 2, 8, BS), F32),
            pltpu.VMEM((BATCH, UNITS, 32, 128), BF16),
            pltpu.VMEM((BATCH, UNITS, 32, 128), BF16),
            pltpu.VMEM((UNITS, 32, 128), BF16),
            pltpu.VMEM((8, 32, 128), BF16),
            pltpu.VMEM((2, 2, UNITS, 32, 128), BF16),
            pltpu.VMEM(tf.shape, BF16),
            pltpu.VMEM(ti.shape, BF16),
            pltpu.VMEM(l1.shape, BF16),
            pltpu.VMEM(l2.shape, BF16),
            pltpu.VMEM(l3.shape, BF16),
            pltpu.SemaphoreType.DMA((5,)),
            pltpu.SemaphoreType.DMA((2, LOCAL)),
            pltpu.SemaphoreType.DMA,
            pltpu.SemaphoreType.DMA((4,)),
            pltpu.SemaphoreType.DMA((3, CHUNKS, n_off)),
            pltpu.SemaphoreType.DMA((3, CHUNKS, n_off)),
            pltpu.SemaphoreType.DMA((3, CHUNKS)),
            pltpu.SemaphoreType.DMA((BATCH,)),
            pltpu.SemaphoreType.DMA((BATCH,)),
            pltpu.SemaphoreType.DMA((UNITS,)),
            pltpu.SemaphoreType.DMA((8,)),
            pltpu.SemaphoreType.DMA((n_off, 2)),
            pltpu.SemaphoreType.DMA((2, 2, UNITS)),
            pltpu.SemaphoreType.DMA((NY,)),
            pltpu.SemaphoreType.DMA((NY,)),
        ],
        compiler_params=pltpu.CompilerParams(
            collective_id=0, has_side_effects=True, vmem_limit_bytes=62 * 1024 * 1024
        ),
        cost_estimate=pl.CostEstimate(flops=10**10, bytes_accessed=10**7, transcendentals=4 * 10**6),
    )(pairs(field), pairs(cotangent), weight_one, bias_one, weight_two, bias_two, tf, ti, l1, l2, l3)

    wshape, bshape = weight_one.shape, bias_one.shape
    field_grad, *rest = pl.pallas_call(
        finish,
        name="finish",
        out_shape=(
            jax.ShapeDtypeStruct((LOCAL, WIDTH, SAMPLES, CH), BF16),
            jax.ShapeDtypeStruct(wshape, F32),
            jax.ShapeDtypeStruct(bshape, F32),
            jax.ShapeDtypeStruct(wshape, F32),
            jax.ShapeDtypeStruct(bshape, F32),
        ),
        in_specs=[hbm] * 3,
        out_specs=[hbm] * 5,
        scratch_shapes=[
            pltpu.VMEM(grecv.shape, BF16),
            pltpu.VMEM((LOCAL, WIDTH, SAMPLES, CH), BF16),
            pltpu.VMEM(every.shape, BF16),
            pltpu.VMEM(tt.shape, BF16),
            pltpu.VMEM(wshape, F32),
            pltpu.VMEM(bshape, F32),
            pltpu.VMEM(wshape, F32),
            pltpu.VMEM(bshape, F32),
            pltpu.SemaphoreType.DMA((LOCAL,)),
            pltpu.SemaphoreType.DMA((LOCAL,)),
            pltpu.SemaphoreType.DMA((6,)),
        ],
        compiler_params=pltpu.CompilerParams(vmem_limit_bytes=62 * 1024 * 1024),
        cost_estimate=pl.CostEstimate(flops=2 * 10**9, bytes_accessed=8 * 10**6, transcendentals=0),
    )(every, grecv, tt)
    return (field_grad.transpose(2, 0, 1, 3), *rest)


def solution(mesh):
    in_specs = (P("batch", "lat", None, None), P("batch", "lat", None, None), P(), P(), P(), P())
    out_specs = (P("batch", "lat", None, None), P(), P(), P(), P())
    return jax.shard_map(local, mesh=mesh, in_specs=in_specs, out_specs=out_specs, check_vma=False)
```

```python
import functools
import math

import jax
import jax.numpy as jnp
import numpy as np
from jax import lax
from jax.experimental import pallas as pl
from jax.experimental.pallas import tpu as pltpu
from jax.sharding import PartitionSpec as P

MESH = pl.DeviceIdType.MESH
F32, BF16 = jnp.float32, jnp.bfloat16
NY = 4
BATCH = 2 * NY
UNITS = 5
KP = 96
QUARTER = 24
JB = 8
CHUNKS = QUARTER // JB
HALF = 384
TILES = HALF // 128
LOCAL = 6
SAMPLES = 2
LAT = 96
WIDTH = 180
CH = 768
BS = 96
ROWS = JB * LAT
RB = ROWS // 2
OFFSETS = [(dx, dz, dc) for dz in (1, 3, 2, 0) for dx in (1, 0) for dc in (1, 0)]
CUTS = (12, 20, 26)
WIN = [(0, 512), (0, 768), (256, 768)]
PIECES = [[(0, 0, 96)], [(0, 96, 128), (1, 0, 64)], [(1, 64, 128), (2, 0, 32)], [(2, 32, 128)]]


def lon_tables():
    wpos, kpos = np.arange(WIDTH), np.arange(KP)
    angle = (wpos[:, None] * kpos[None, :] % WIDTH).astype(np.float32) * np.float32(2.0 * math.pi / WIDTH)
    valid = (kpos <= WIDTH // 2).astype(np.float32)[None, :]
    factor = np.float32(1.0 / math.sqrt(WIDTH))
    cosine, sine = np.cos(angle) * valid * factor, np.sin(angle) * valid * factor
    weight = np.where((kpos == 0) | (kpos == WIDTH // 2), 1.0, 2.0).astype(np.float32)[None, :]

    def rows(real, imag):
        both = np.stack([real.T, imag.T]).reshape(2, 4, CHUNKS, JB, WIDTH)
        return both.transpose(1, 2, 0, 3, 4).reshape(2 * KP, WIDTH).astype(BF16)

    def paired(table):
        both = np.zeros((SAMPLES, 2 * KP, WIDTH, SAMPLES), BF16)
        for s in range(SAMPLES):
            both[s, :, :, s] = table
        return both.reshape(SAMPLES * 2 * KP, WIDTH * SAMPLES)

    return paired(rows(cosine, -sine)), paired(rows(cosine * weight, -sine * weight))


def lat_tables():
    pos = np.arange(LAT)
    angle = (pos[:, None] * pos[None, :] % LAT).astype(np.float32) * np.float32(2.0 * math.pi / LAT)
    factor = np.float32(1.0 / math.sqrt(LAT))
    cosine = np.cos(angle) * factor

    def real_form(sign):
        sine = np.sin(angle) * np.float32(factor * sign)
        return np.stack([np.stack([cosine, -sine], -1), np.stack([sine, cosine], -1)], 1).astype(BF16)

    fwd = real_form(-1.0).transpose(1, 0, 3, 2).reshape(2 * LAT, 2 * LAT)
    inv = real_form(1.0).transpose(3, 2, 1, 0).reshape(2 * LAT, 2 * LAT)
    return fwd, inv, np.ascontiguousarray(fwd.T)


def dot(a, b):
    return jnp.dot(a, b, preferred_element_type=F32)


def dot_tb(a, b):
    return lax.dot_general(a, b, (((1,), (1,)), ((), ())), preferred_element_type=F32)


def dot_ta(a, b):
    return lax.dot_general(a, b, (((0,), (0,)), ((), ())), preferred_element_type=F32)


def kernel(
    field, cot, w1, b1, w2, b2, tf_hbm, ti_hbm, l1_hbm, l2_hbm, l3_hbm,
    grecv, every,
    slab, send, recv, gsend, mixed, hidden, slope, mask, dsec, dfir, scr, bmat, wm, wtmp, bias, acc, gb,
    wraw, braw, packed, parts, shares, pieces, done, tf, ti, l1, l2, l3,
    table_sem, slab_sem, every_sem, par_sem, ssem, rsem, own_sem, rs_s, rs_r, sum_s, sum_r, all_s, all_r, ag_s, ag_r, pass_s, pass_r, early_s, early_r,
):
    batch, me = lax.axis_index("batch"), lax.axis_index("lat")
    half, zz, core = me // 8, (me // 2) % 4, me % 2
    side, yy = batch // NY, batch % NY
    other = (1 - side) * NY + yy

    def along(o):
        return side * NY + (yy + o) % NY

    def partner(o):
        dx, dz, dc = o
        return (half + dx) % 2, (zz + dz) % 4, (core + dc) % 2

    def index(part):
        return part[0] * 8 + part[1] * 2 + part[2]

    def source(o):
        dx, dz, dc = o
        return ((half + dx) % 2) * 8 + ((zz + 4 - dz) % 4) * 2 + (core + dc) % 2

    def slab_copy(a, h):
        return pltpu.make_async_copy((field, cot)[a].at[h], slab.at[a, h], slab_sem.at[a, h])

    tables = [
        pltpu.make_async_copy(src, dst, table_sem.at[i])
        for i, (src, dst) in enumerate(((tf_hbm, tf), (ti_hbm, ti), (l1_hbm, l1), (l2_hbm, l2), (l3_hbm, l3)))
    ]
    tables[0].start()
    for h in range(LOCAL):
        slab_copy(0, h).start()
    for copy in tables[1:]:
        copy.start()
    params = [
        pltpu.make_async_copy(w1.at[:, pl.ds(half * 4, 4)], wraw.at[0], par_sem.at[0]),
        pltpu.make_async_copy(w2.at[:, pl.ds(half * 4, 4)], wraw.at[1], par_sem.at[1]),
        pltpu.make_async_copy(b1, braw.at[0], par_sem.at[2]),
        pltpu.make_async_copy(b2, braw.at[1], par_sem.at[3]),
    ]
    for copy in params:
        copy.start()

    barrier = pltpu.get_barrier_semaphore()
    for o in OFFSETS:
        if o != (0, 0, 0):
            pl.semaphore_signal(barrier, inc=1, device_id=(batch, index(partner(o))), device_id_type=MESH)
        pl.semaphore_signal(barrier, inc=1, device_id=(other, index(partner(o))), device_id_type=MESH)
    for o in range(1, NY):
        for to in (along(o), (1 - side) * NY + (yy + o) % NY):
            pl.semaphore_signal(barrier, inc=1, device_id=(to, me), device_id_type=MESH)

    def lanes(part):
        return pl.ds(pl.multiple_of(part * HALF, 128), HALF)

    def rows16(sample, quarter, jc):
        return pl.ds(pl.multiple_of(sample * 2 * KP + quarter * 48 + jc * 16, 16), 16)

    def chunk(jc):
        return pl.ds(pl.multiple_of(jc * 16, 16), 16)

    def early(part, i):
        to = partner(OFFSETS[i])
        here = pl.ds(part * (LOCAL // 2), LOCAL // 2)
        src = send.at[0, here, rows16(to[2], to[1], 0), lanes(to[0])]
        dst = recv.at[0, me, here, chunk(0), :]
        if OFFSETS[i] == (0, 0, 0):
            return pltpu.make_async_copy(src, dst, early_s.at[i + part])
        sems = (early_s.at[i], early_r.at[i]) if part == 0 else (ssem.at[0, 0, i], rsem.at[0, 0, i])
        return pltpu.make_async_remote_copy(
            src, dst, *sems, device_id=(batch, index(to)), device_id_type=MESH
        )

    def early_wait(i):
        for part in range(2):
            if OFFSETS[i] == (0, 0, 0):
                early(part, i).wait()
                continue
            dst = recv.at[0, source(OFFSETS[i]), pl.ds(part * (LOCAL // 2), LOCAL // 2), chunk(0), :]
            sems = (early_s.at[i], early_r.at[i]) if part == 0 else (ssem.at[0, 0, i], rsem.at[0, 0, i])
            pltpu.make_async_remote_copy(
                dst, dst, *sems, device_id=(batch, me), device_id_type=MESH
            ).wait_recv()

    def inward(a, jc, i):
        to = partner(OFFSETS[i])
        src = send.at[a, :, rows16(to[2], to[1], jc), lanes(to[0])]
        dst = recv.at[a, me, :, chunk(jc), :]
        if OFFSETS[i] == (0, 0, 0):
            return pltpu.make_async_copy(src, dst, own_sem.at[a, jc])
        return pltpu.make_async_remote_copy(
            src, dst, ssem.at[a, jc, i], rsem.at[a, jc, i], device_id=(batch, index(to)), device_id_type=MESH
        )

    def inward_wait(a, jc, i):
        if OFFSETS[i] == (0, 0, 0):
            inward(a, jc, i).wait()
            return
        dst = recv.at[a, source(OFFSETS[i]), :, chunk(jc), :]
        pltpu.make_async_remote_copy(
            dst, dst, ssem.at[a, jc, i], rsem.at[a, jc, i], device_id=(batch, me), device_id_type=MESH
        ).wait_recv()

    def outward(jc, i):
        to = index(partner(OFFSETS[i]))
        src = gsend.at[pl.ds(to * LOCAL, LOCAL), chunk(jc), :]
        dst = grecv.at[:, rows16(core, zz, jc), lanes(half)]
        if OFFSETS[i] == (0, 0, 0):
            return pltpu.make_async_copy(src, dst, own_sem.at[2, jc])
        return pltpu.make_async_remote_copy(
            src, dst, ssem.at[2, jc, i], rsem.at[2, jc, i], device_id=(batch, to), device_id_type=MESH
        )

    def outward_wait(jc, i):
        if OFFSETS[i] == (0, 0, 0):
            outward(jc, i).wait()
            return
        dx, dz, dc = OFFSETS[i]
        fx, fz, fc = (half + dx) % 2, (zz + 4 - dz) % 4, (core + dc) % 2
        dst = grecv.at[:, rows16(fc, fz, jc), lanes(fx)]
        pltpu.make_async_remote_copy(
            dst, dst, ssem.at[2, jc, i], rsem.at[2, jc, i], device_id=(batch, me), device_id_type=MESH
        ).wait_recv()

    def longitude(a, first=0, last=LOCAL):
        table = (tf, ti)[a]

        def one(h, carry):
            slab_copy(a, h).wait()
            if a == 0:
                slab_copy(1, h).start()
            pair = slab[a, h].reshape(WIDTH * SAMPLES, CH)
            send[a, h] = dot(table[...], pair).astype(BF16)
            return carry

        lax.fori_loop(first, last, one, 0)

    tables[0].wait()
    longitude(0, 0, LOCAL // 2)
    pl.semaphore_wait(barrier, 2 * len(OFFSETS) - 1 + 2 * (NY - 1))
    for i in range(len(OFFSETS)):
        early(0, i).start()
    longitude(0, LOCAL // 2, LOCAL)
    for i in range(len(OFFSETS)):
        early(1, i).start()
    for jc in range(1, CHUNKS):
        for i in range(len(OFFSETS)):
            inward(0, jc, i).start()
    tables[1].wait()
    longitude(1)
    for jc in range(CHUNKS):
        for i in range(len(OFFSETS)):
            inward(1, jc, i).start()

    for copy in params + tables[2:]:
        copy.wait()
    row_id = lax.broadcasted_iota(jnp.int32, (BS, HALF), 0)
    col_id = lax.broadcasted_iota(jnp.int32, (BS, HALF), 1)
    for w in range(2):
        for part in range(2):
            total = jnp.zeros((8, HALF), F32)
            for n in range(4):
                place = jnp.where(row_id + n * BS == col_id, 1.0, 0.0).astype(F32)
                placed = dot(wraw[w, part, n].astype(BF16), place.astype(BF16))
                wtmp[part, n * BS : (n + 1) * BS, :] = placed.astype(BF16)
                line = jnp.broadcast_to(braw[w, part, pl.ds(half * 4 + n, 1), :], (8, BS))
                total = total + jnp.dot(line, place, precision=lax.Precision.HIGHEST, preferred_element_type=F32)
            for t in range(TILES):
                c = (2 * t + part) * 128
                bias[w, :, c : c + 128] = total[:, t * 128 : (t + 1) * 128]
        for t in range(TILES):
            for u in range(TILES):
                real = wtmp[0, t * 128 : (t + 1) * 128, u * 128 : (u + 1) * 128]
                imag = wtmp[1, t * 128 : (t + 1) * 128, u * 128 : (u + 1) * 128]
                r, c = t * 256, u * 256
                wm[w, r : r + 128, c : c + 128] = real
                wm[w, r : r + 128, c + 128 : c + 256] = imag
                wm[w, r + 128 : r + 256, c : c + 128] = -imag
                wm[w, r + 128 : r + 256, c + 128 : c + 256] = real
    acc[...] = jnp.zeros_like(acc)
    gb[...] = jnp.zeros_like(gb)

    def gather(a, jc):
        if a == 0:

            @pl.when(jc == 0)
            def _():
                for i in range(len(OFFSETS)):
                    early_wait(i)

            @pl.when(jc > 0)
            def _():
                for i in range(len(OFFSETS)):
                    inward_wait(a, jc, i)

        else:
            for i in range(len(OFFSETS)):
                inward_wait(a, jc, i)

        def one(l, carry):
            rows = recv[a, l, :, chunk(jc), :].astype(F32).reshape(LOCAL * 16, HALF)
            for t in range(TILES):
                scr[t, pl.ds(pl.multiple_of(l * 96, 8), 96), :] = rows[:, t * 128 : (t + 1) * 128]
            return carry

        lax.fori_loop(0, 16, one, 0)

    def column(j):
        parts = [
            jnp.concatenate([scr[t, pl.ds(q * JB + j, LAT, stride=16), :] for t in range(TILES)], axis=1)
            for q in range(2)
        ]
        return jnp.concatenate(parts, axis=0).astype(BF16)

    def row_block(jc, rb):
        return pl.ds(pl.multiple_of(jc * ROWS + rb * RB, 128), RB)

    def forward(jc, carry):
        gather(0, jc)

        def one(j, c):
            res = dot(l1[...], column(j))
            rows = pl.ds(pl.multiple_of(jc * ROWS + j * LAT, 32), LAT)
            for p in range(2):
                for t in range(TILES):
                    mixed[rows, (2 * t + p) * 128 : (2 * t + p + 1) * 128] = res[
                        p * LAT : (p + 1) * LAT, t * 128 : (t + 1) * 128
                    ].astype(BF16)
            return c

        lax.fori_loop(0, JB, one, 0)

        def mix(rb, c):
            rows = row_block(jc, rb)
            for t in range(TILES):
                lo, hi = WIN[t]
                cols = slice(t * 256, (t + 1) * 256)
                x = dot(mixed[rows, lo:hi], wm[0, lo:hi, cols]) + bias[0, 0:1, cols]
                c0, c1 = math.sqrt(2.0 / math.pi), 0.044715
                xx = x * x
                th = jnp.tanh(x * (c0 + (c0 * c1) * xx))
                gate = 0.5 + 0.5 * th
                hidden[rows, cols] = (x * gate).astype(BF16)
                rise = (0.5 * x) * (1.0 - th * th) * (c0 + (3.0 * c0 * c1) * xx)
                slope[rows, cols] = (gate + rise).astype(BF16)
            for t in range(TILES):
                lo, hi = WIN[t]
                cols = slice(t * 256, (t + 1) * 256)
                y = dot(hidden[rows, lo:hi], wm[1, lo:hi, cols]) + bias[1, 0:1, cols]
                th = jnp.tanh(4.0 * y)
                mask[rows, cols] = (th * th).astype(BF16)
            return c

        lax.fori_loop(0, 2, mix, 0)
        return carry

    lax.fori_loop(0, CHUNKS, forward, 0)

    def to_hidden(jc):
        gather(1, jc)

        def one(j, c):
            res = dot(l2[...], column(j)).astype(BF16)
            rows = pl.ds(pl.multiple_of(jc * ROWS + j * LAT, 32), LAT)
            here = pl.ds(pl.multiple_of(j * LAT, 32), LAT)
            for p in range(2):
                for t in range(TILES):
                    cols = slice((2 * t + p) * 128, (2 * t + p + 1) * 128)
                    part = res[p * LAT : (p + 1) * LAT, t * 128 : (t + 1) * 128].astype(F32)
                    dsec[here, cols] = (part * mask[rows, cols].astype(F32)).astype(BF16)
            return c

        lax.fori_loop(0, JB, one, 0)

        def mix(rb, c):
            rows = row_block(jc, rb)
            here = pl.ds(pl.multiple_of(rb * RB, 128), RB)
            for t in range(TILES):
                lo, hi = WIN[t]
                cols = slice(t * 256, (t + 1) * 256)
                d = dot_tb(dsec[here, lo:hi], wm[1, cols, lo:hi])
                dfir[here, cols] = (d * slope[rows, cols].astype(F32)).astype(BF16)
            return c

        lax.fori_loop(0, 2, mix, 0)

    def to_spectra(jc):
        def mix(rb, c):
            here = pl.ds(pl.multiple_of(rb * RB, 128), RB)
            for t in range(TILES):
                lo, hi = WIN[t]
                cols = slice(t * 256, (t + 1) * 256)
                d = dot_tb(dfir[here, lo:hi], wm[0, cols, lo:hi]).astype(BF16)
                for jl in range(JB // 2):
                    for p in range(2):
                        bmat[rb * (JB // 2) + jl, p * LAT : (p + 1) * LAT, t * 128 : (t + 1) * 128] = d[
                            jl * LAT : (jl + 1) * LAT, p * 128 : (p + 1) * 128
                        ]
            return c

        lax.fori_loop(0, 2, mix, 0)

        def last(j, c):
            res = dot(l3[...], bmat[j])
            for q in range(2):
                for t in range(TILES):
                    scr[t, pl.ds(q * JB + j, LAT, stride=16), :] = res[
                        q * LAT : (q + 1) * LAT, t * 128 : (t + 1) * 128
                    ]
            return c

        lax.fori_loop(0, JB, last, 0)

        def pack(l, c):
            for t in range(TILES):
                part = scr[t, pl.ds(pl.multiple_of(l * 96, 8), 96), :]
                gsend[pl.ds(l * LOCAL, LOCAL), chunk(jc), t * 128 : (t + 1) * 128] = part.astype(BF16).reshape(
                    LOCAL, 16, 128
                )
            return c

        lax.fori_loop(0, 16, pack, 0)

    def to_weights(jc):
        here = pl.ds(pl.multiple_of(jc * ROWS, 128), ROWS)
        for t in range(TILES):
            lo, hi = WIN[t]
            cols = slice(t * 256, (t + 1) * 256)
            acc[1, cols, lo:hi] += dot_ta(hidden[here, cols], dsec[:, lo:hi])
            acc[0, cols, lo:hi] += dot_ta(mixed[here, cols], dfir[:, lo:hi])
        ones = jnp.ones((16, ROWS), BF16)
        gb[0] += dot(ones, dfir[...])[0:8]
        gb[1] += dot(ones, dsec[...])[0:8]

    def backward(jc, carry):
        to_hidden(jc)
        to_spectra(jc)

        @pl.when(jc < 1)
        def _():
            for i in range(len(OFFSETS)):
                outward(jc, i).start()

        to_weights(jc)
        return carry

    lax.fori_loop(0, CHUNKS - 1, backward, 0)
    to_hidden(CHUNKS - 1)
    to_weights(CHUNKS - 1)

    lane = lax.broadcasted_iota(jnp.int32, (BS, 128), 1)
    for w in range(2):
        for part in range(2):
            for t in range(TILES):

                def block(n):
                    found = []
                    for u, lo, hi in PIECES[n]:
                        r, c = u * 256, t * 256
                        top = acc[w, r + lo : r + hi, c + part * 128 : c + (part + 1) * 128]
                        low = acc[w, r + 128 + lo : r + 128 + hi, c + (1 - part) * 128 : c + (2 - part) * 128]
                        found.append(top + low if part == 0 else top - low)
                    return found[0] if len(found) == 1 else jnp.concatenate(found, axis=0)

                tile = jnp.where(lane < 96 - 32 * t, block(t), block(t + 1)).astype(BF16)
                for i in range(3):
                    u = ((w * 2 + part) * TILES + t) * 3 + i
                    packed[u // UNITS, u % UNITS] = tile[i * 32 : (i + 1) * 32]
    row = lax.broadcasted_iota(jnp.int32, (32, 128), 0)
    lines = jnp.zeros((32, 128), F32)
    for w in range(2):
        for part in range(2):
            for t in range(TILES):
                line = gb[w, 0:1, (2 * t + part) * 128 : (2 * t + part + 1) * 128]
                lines = jnp.where(row == (w * 2 + part) * TILES + t, jnp.broadcast_to(line, (32, 128)), lines)
    packed[7, 1] = lines.astype(BF16)
    for u in range(2, UNITS):
        packed[7, u] = jnp.zeros((32, 128), BF16)

    def share(o):
        return pltpu.make_async_remote_copy(
            packed.at[(batch + o) % BATCH], parts.at[batch], rs_s.at[o], rs_r.at[o],
            device_id=((batch + o) % BATCH, me), device_id_type=MESH,
        )

    for o in range(1, BATCH):
        share(o).start()
    back = [(jc, i) for jc in range(1, CHUNKS) for i in range(len(OFFSETS))]
    for jc, i in back[:CUTS[0]]:
        outward(jc, i).start()
    to_spectra(CHUNKS - 1)
    parts[batch] = packed[batch]
    for o in range(1, BATCH):
        dst = parts.at[(batch + BATCH - o) % BATCH]
        pltpu.make_async_remote_copy(
            dst, dst, rs_s.at[o], rs_r.at[o], device_id=(batch, me), device_id_type=MESH
        ).wait_recv()
    total = parts[0].astype(F32)
    for o in range(1, BATCH):
        total = total + parts[o].astype(F32)
    shares[...] = total.astype(BF16)

    mine = me % 8

    def to_reducer(g):
        return pltpu.make_async_remote_copy(
            shares.at[g], pieces.at[mine], sum_s.at[g], sum_r.at[mine],
            device_id=(batch, half * 8 + g), device_id_type=MESH,
        )

    def to_all(i, far):
        return pltpu.make_async_remote_copy(
            done.at[side, half, mine], done.at[side, half, mine], all_s.at[i, far], all_r.at[side, half, mine],
            device_id=((batch, other)[far], index(partner(OFFSETS[i]))), device_id_type=MESH,
        )

    listeners = [(i, far) for i, o in enumerate(OFFSETS) for far in range(2) if (o, far) != ((0, 0, 0), 0)]
    for g in range(UNITS):

        @pl.when(mine != g)
        def _(g=g):
            to_reducer(g).start()

    for jc, i in back[CUTS[0] : CUTS[1]]:
        outward(jc, i).start()

    @pl.when(mine < UNITS)
    def _():
        pieces[mine] = shares[mine]
        for g in range(8):

            @pl.when(mine != g)
            def _(g=g):
                dst = pieces.at[g]
                pltpu.make_async_remote_copy(
                    dst, dst, sum_s.at[0], sum_r.at[g], device_id=(batch, me), device_id_type=MESH
                ).wait_recv()

        whole = pieces[0].astype(F32)
        for g in range(1, 8):
            whole = whole + pieces[g].astype(F32)
        samples = SAMPLES * 2 * NY
        done[side, half, mine] = (whole * (1.0 / math.sqrt(samples * LAT * (WIDTH // 2 + 1)))).astype(BF16)
        for i, far in listeners:
            to_all(i, far).start()

    for jc, i in back[CUTS[1] : CUTS[2]]:
        outward(jc, i).start()

    for sd in range(2):
        for hf in range(2):
            for g in range(UNITS):

                @pl.when((side != sd) | (half != hf) | (mine != g))
                def _(sd=sd, hf=hf, g=g):
                    dst = done.at[sd, hf, g]
                    pltpu.make_async_remote_copy(
                        dst, dst, all_s.at[0, 0], all_r.at[sd, hf, g], device_id=(batch, me), device_id_type=MESH
                    ).wait_recv()

    def gathered(o):
        return pltpu.make_async_remote_copy(
            done.at[core], every.at[yy, core], ag_s.at[o], ag_r.at[o],
            device_id=(along(o), me), device_id_type=MESH,
        )

    def passed(o):
        got = every.at[(yy + NY - o) % NY, core]
        return pltpu.make_async_remote_copy(
            got, got, pass_s.at[o], pass_r.at[o], device_id=(batch, me + 1 - 2 * core), device_id_type=MESH
        )

    for o in range(1, NY):
        gathered(o).start()
    kept = pltpu.make_async_copy(done, every.at[yy], every_sem)
    kept.start()
    for jc, i in back[CUTS[2] :]:
        outward(jc, i).start()

    for o in range(1, NY):
        dst = every.at[(yy + NY - o) % NY, core]
        pltpu.make_async_remote_copy(
            dst, dst, ag_s.at[o], ag_r.at[o], device_id=(batch, me), device_id_type=MESH
        ).wait_recv()
        passed(o).start()
    for jc in range(CHUNKS):
        for i in range(len(OFFSETS)):
            outward_wait(jc, i)
    for o in range(1, NY):
        dst = every.at[(yy + NY - o) % NY, 1 - core]
        pltpu.make_async_remote_copy(
            dst, dst, pass_s.at[o], pass_r.at[o], device_id=(batch, me), device_id_type=MESH
        ).wait_recv()
    kept.wait()

    for o in range(1, BATCH):
        share(o).wait_send()
    for o in range(1, NY):
        gathered(o).wait_send()
        passed(o).wait_send()
    for g in range(UNITS):

        @pl.when(mine != g)
        def _(g=g):
            to_reducer(g).wait_send()

    @pl.when(mine < UNITS)
    def _():
        for i, far in listeners:
            to_all(i, far).wait_send()

    for a in range(3):
        for jc in range(CHUNKS):
            for i, o in enumerate(OFFSETS):
                if o != (0, 0, 0) and (a, jc) == (0, 0):
                    early(0, i).wait_send()
                    early(1, i).wait_send()
                elif o != (0, 0, 0):
                    (outward(jc, i) if a == 2 else inward(a, jc, i)).wait_send()


def finish(
    every, grecv, tt, out, gw1_hbm, gb1_hbm, gw2_hbm, gb2_hbm,
    slab, pair, sums, table, gw1, gb1, gw2, gb2, in_sem, out_sem, par_sem,
):
    fetch = [pltpu.make_async_copy(tt, table, par_sem.at[0]), pltpu.make_async_copy(every, sums, par_sem.at[1])]
    fetch[1].start()
    fetch[0].start()
    for h in range(LOCAL):
        pltpu.make_async_copy(grecv.at[h], slab.at[h], in_sem.at[h]).start()
    fetch[1].wait()
    for w, gw, gbias in ((0, gw1, gb1), (1, gw2, gb2)):
        for part in range(2):
            for hf in range(2):
                tiles, lines = [], []
                for t in range(TILES):
                    k = (w * 2 + part) * TILES + t
                    found = [sums[u // UNITS % NY, u // UNITS // NY, hf, u % UNITS] for u in range(3 * k, 3 * k + 3)]
                    tiles.append(jnp.concatenate(found, axis=0).astype(F32))
                    lines.append(jnp.broadcast_to(sums[3, 1, hf, 1].astype(F32)[k : k + 1], (8, 128)))

                def blocks(x, n):
                    if n == 0:
                        return x[0][:, :BS]
                    if n == 3:
                        return pltpu.roll(x[2], BS, 1)[:, :BS]
                    return pltpu.roll(jnp.concatenate(x[n - 1 : n + 1], axis=1), 128 + 32 * n, 1)[:, :BS]

                for n in range(4):
                    gw[part, hf * 4 + n] = blocks(tiles, n)
                    gbias[part, hf * 4 + n : hf * 4 + n + 1, :] = blocks(lines, n)[0:1]
    outs = [
        pltpu.make_async_copy(src, dst, par_sem.at[2 + i])
        for i, (src, dst) in enumerate(((gw1, gw1_hbm), (gb1, gb1_hbm), (gw2, gw2_hbm), (gb2, gb2_hbm)))
    ]
    for copy in outs:
        copy.start()
    fetch[0].wait()

    def one(h, carry):
        pltpu.make_async_copy(grecv.at[h], slab.at[h], in_sem.at[h]).wait()
        pair[h] = dot(table[...], slab[h]).astype(BF16).reshape(WIDTH, SAMPLES, CH)
        pltpu.make_async_copy(pair.at[h], out.at[h], out_sem.at[h]).start()
        return carry

    lax.fori_loop(0, LOCAL, one, 0)
    for copy in outs:
        copy.wait()
    for h in range(LOCAL):
        pltpu.make_async_copy(pair.at[h], out.at[h], out_sem.at[h]).wait()


def local(field, cotangent, weight_one, bias_one, weight_two, bias_two):
    tf, ti = lon_tables()
    tt = np.ascontiguousarray(tf.T)
    l1, l2, l3 = lat_tables()
    hbm = pl.BlockSpec(memory_space=pl.ANY)
    n_off = len(OFFSETS)

    def pairs(x):
        return x.transpose(1, 2, 0, 3)

    grecv, every = pl.pallas_call(
        kernel,
        name="afno_backward",
        out_shape=(
            jax.ShapeDtypeStruct((LOCAL, SAMPLES * 2 * KP, CH), BF16),
            jax.ShapeDtypeStruct((NY, 2, 2, UNITS, 32, 128), BF16),
        ),
        in_specs=[hbm] * 11,
        out_specs=(hbm, hbm),
        scratch_shapes=[
            pltpu.VMEM((2, LOCAL, WIDTH, SAMPLES, CH), BF16),
            pltpu.VMEM((2, LOCAL, SAMPLES * 2 * KP, CH), BF16),
            pltpu.VMEM((2, 16, LOCAL, 2 * QUARTER, HALF), BF16),
            pltpu.VMEM((LAT, 2 * QUARTER, HALF), BF16),
            pltpu.VMEM((CHUNKS * ROWS, CH), BF16),
            pltpu.VMEM((CHUNKS * ROWS, CH), BF16),
            pltpu.VMEM((CHUNKS * ROWS, CH), BF16),
            pltpu.VMEM((CHUNKS * ROWS, CH), BF16),
            pltpu.VMEM((ROWS, CH), BF16),
            pltpu.VMEM((ROWS, CH), BF16),
            pltpu.VMEM((TILES, LAT * 16, 128), F32),
            pltpu.VMEM((JB, 2 * LAT, HALF), BF16),
            pltpu.VMEM((2, CH, CH), BF16),
            pltpu.VMEM((2, HALF, HALF), BF16),
            pltpu.VMEM((2, 8, CH), F32),
            pltpu.VMEM((2, CH, CH), F32),
            pltpu.VMEM((2, 8, CH), F32),
            pltpu.VMEM((2, 2, 4, BS, BS), F32),
            pltpu.VMEM((2, 2, 8, BS), F32),
            pltpu.VMEM((BATCH, UNITS, 32, 128), BF16),
            pltpu.VMEM((BATCH, UNITS, 32, 128), BF16),
            pltpu.VMEM((UNITS, 32, 128), BF16),
            pltpu.VMEM((8, 32, 128), BF16),
            pltpu.VMEM((2, 2, UNITS, 32, 128), BF16),
            pltpu.VMEM(tf.shape, BF16),
            pltpu.VMEM(ti.shape, BF16),
            pltpu.VMEM(l1.shape, BF16),
            pltpu.VMEM(l2.shape, BF16),
            pltpu.VMEM(l3.shape, BF16),
            pltpu.SemaphoreType.DMA((5,)),
            pltpu.SemaphoreType.DMA((2, LOCAL)),
            pltpu.SemaphoreType.DMA,
            pltpu.SemaphoreType.DMA((4,)),
            pltpu.SemaphoreType.DMA((3, CHUNKS, n_off)),
            pltpu.SemaphoreType.DMA((3, CHUNKS, n_off)),
            pltpu.SemaphoreType.DMA((3, CHUNKS)),
            pltpu.SemaphoreType.DMA((BATCH,)),
            pltpu.SemaphoreType.DMA((BATCH,)),
            pltpu.SemaphoreType.DMA((UNITS,)),
            pltpu.SemaphoreType.DMA((8,)),
            pltpu.SemaphoreType.DMA((n_off, 2)),
            pltpu.SemaphoreType.DMA((2, 2, UNITS)),
            pltpu.SemaphoreType.DMA((NY,)),
            pltpu.SemaphoreType.DMA((NY,)),
            pltpu.SemaphoreType.DMA((NY,)),
            pltpu.SemaphoreType.DMA((NY,)),
            pltpu.SemaphoreType.DMA((n_off + 1,)),
            pltpu.SemaphoreType.DMA((n_off,)),
        ],
        compiler_params=pltpu.CompilerParams(
            collective_id=0, has_side_effects=True, vmem_limit_bytes=62 * 1024 * 1024
        ),
        cost_estimate=pl.CostEstimate(flops=10**10, bytes_accessed=10**7, transcendentals=4 * 10**6),
    )(pairs(field), pairs(cotangent), weight_one, bias_one, weight_two, bias_two, tf, ti, l1, l2, l3)

    wshape, bshape = weight_one.shape, bias_one.shape
    field_grad, *rest = pl.pallas_call(
        finish,
        name="finish",
        out_shape=(
            jax.ShapeDtypeStruct((LOCAL, WIDTH, SAMPLES, CH), BF16),
            jax.ShapeDtypeStruct(wshape, F32),
            jax.ShapeDtypeStruct(bshape, F32),
            jax.ShapeDtypeStruct(wshape, F32),
            jax.ShapeDtypeStruct(bshape, F32),
        ),
        in_specs=[hbm] * 3,
        out_specs=[hbm] * 5,
        scratch_shapes=[
            pltpu.VMEM(grecv.shape, BF16),
            pltpu.VMEM((LOCAL, WIDTH, SAMPLES, CH), BF16),
            pltpu.VMEM(every.shape, BF16),
            pltpu.VMEM(tt.shape, BF16),
            pltpu.VMEM(wshape, F32),
            pltpu.VMEM(bshape, F32),
            pltpu.VMEM(wshape, F32),
            pltpu.VMEM(bshape, F32),
            pltpu.SemaphoreType.DMA((LOCAL,)),
            pltpu.SemaphoreType.DMA((LOCAL,)),
            pltpu.SemaphoreType.DMA((6,)),
        ],
        compiler_params=pltpu.CompilerParams(vmem_limit_bytes=62 * 1024 * 1024),
        cost_estimate=pl.CostEstimate(flops=2 * 10**9, bytes_accessed=8 * 10**6, transcendentals=0),
    )(every, grecv, tt)
    return (field_grad.transpose(2, 0, 1, 3), *rest)


def solution(mesh):
    in_specs = (P("batch", "lat", None, None), P("batch", "lat", None, None), P(), P(), P(), P())
    out_specs = (P("batch", "lat", None, None), P(), P(), P(), P())
    return jax.shard_map(local, mesh=mesh, in_specs=in_specs, out_specs=out_specs, check_vma=False)
```

```python
import functools
import math

import jax
import jax.numpy as jnp
import numpy as np
from jax import lax
from jax.experimental import pallas as pl
from jax.experimental.pallas import tpu as pltpu
from jax.sharding import PartitionSpec as P

MESH = pl.DeviceIdType.MESH
F32, BF16 = jnp.float32, jnp.bfloat16
NY = 4
BATCH = 2 * NY
UNITS = 5
KP = 96
QUARTER = 24
JB = 8
CHUNKS = QUARTER // JB
HALF = 384
TILES = HALF // 128
LOCAL = 6
SAMPLES = 2
LAT = 96
WIDTH = 180
CH = 768
BS = 96
ROWS = JB * LAT
RB = ROWS // 2
OFFSETS = [(dx, dz, dc) for dz in (1, 3, 2, 0) for dx in (1, 0) for dc in (1, 0)]
CUTS = (12, 20, 26)
WIN = [(0, 512), (0, 768), (256, 768)]
PIECES = [[(0, 0, 96)], [(0, 96, 128), (1, 0, 64)], [(1, 64, 128), (2, 0, 32)], [(2, 32, 128)]]


def lon_tables():
    wpos, kpos = np.arange(WIDTH), np.arange(KP)
    angle = (wpos[:, None] * kpos[None, :] % WIDTH).astype(np.float32) * np.float32(2.0 * math.pi / WIDTH)
    valid = (kpos <= WIDTH // 2).astype(np.float32)[None, :]
    factor = np.float32(1.0 / math.sqrt(WIDTH))
    cosine, sine = np.cos(angle) * valid * factor, np.sin(angle) * valid * factor
    weight = np.where((kpos == 0) | (kpos == WIDTH // 2), 1.0, 2.0).astype(np.float32)[None, :]

    def rows(real, imag):
        both = np.stack([real.T, imag.T]).reshape(2, 4, CHUNKS, JB, WIDTH)
        return both.transpose(1, 2, 0, 3, 4).reshape(2 * KP, WIDTH).astype(BF16)

    def paired(table):
        both = np.zeros((SAMPLES, 2 * KP, WIDTH, SAMPLES), BF16)
        for s in range(SAMPLES):
            both[s, :, :, s] = table
        return both.reshape(SAMPLES * 2 * KP, WIDTH * SAMPLES)

    return paired(rows(cosine, -sine)), paired(rows(cosine * weight, -sine * weight))


def lat_tables():
    pos = np.arange(LAT)
    angle = (pos[:, None] * pos[None, :] % LAT).astype(np.float32) * np.float32(2.0 * math.pi / LAT)
    factor = np.float32(1.0 / math.sqrt(LAT))
    cosine = np.cos(angle) * factor

    def real_form(sign):
        sine = np.sin(angle) * np.float32(factor * sign)
        return np.stack([np.stack([cosine, -sine], -1), np.stack([sine, cosine], -1)], 1).astype(BF16)

    fwd = real_form(-1.0).transpose(1, 0, 3, 2).reshape(2 * LAT, 2 * LAT)
    inv = real_form(1.0).transpose(3, 2, 1, 0).reshape(2 * LAT, 2 * LAT)
    return fwd, inv, np.ascontiguousarray(fwd.T)


def dot(a, b):
    return jnp.dot(a, b, preferred_element_type=F32)


def dot_tb(a, b):
    return lax.dot_general(a, b, (((1,), (1,)), ((), ())), preferred_element_type=F32)


def dot_ta(a, b):
    return lax.dot_general(a, b, (((0,), (0,)), ((), ())), preferred_element_type=F32)


def kernel(
    field, cot, w1, b1, w2, b2, tf_hbm, ti_hbm, l1_hbm, l2_hbm, l3_hbm,
    grecv, every,
    slab, send, recv, gsend, mixed, hidden, slope, mask, dsec, dfir, scr, bmat, wm, wtmp, bias, acc, gb,
    wraw, braw, packed, parts, shares, pieces, done, tf, ti, l1, l2, l3,
    table_sem, slab_sem, every_sem, par_sem, ssem, rsem, rs_s, rs_r, sum_s, sum_r, all_s, all_r, ag_s, ag_r, pass_s, pass_r,
):
    batch, me = lax.axis_index("batch"), lax.axis_index("lat")
    half, zz, core = me // 8, (me // 2) % 4, me % 2
    side, yy = batch // NY, batch % NY
    other = (1 - side) * NY + yy

    def along(o):
        return side * NY + (yy + o) % NY

    def partner(o):
        dx, dz, dc = o
        return (half + dx) % 2, (zz + dz) % 4, (core + dc) % 2

    def index(part):
        return part[0] * 8 + part[1] * 2 + part[2]

    def slab_copy(a, h):
        return pltpu.make_async_copy((field, cot)[a].at[h], slab.at[a, h], slab_sem.at[a, h])

    tables = [
        pltpu.make_async_copy(src, dst, table_sem.at[i])
        for i, (src, dst) in enumerate(((tf_hbm, tf), (ti_hbm, ti), (l1_hbm, l1), (l2_hbm, l2), (l3_hbm, l3)))
    ]
    tables[0].start()
    for h in range(LOCAL):
        slab_copy(0, h).start()
    for copy in tables[1:]:
        copy.start()
    params = [
        pltpu.make_async_copy(w1.at[:, pl.ds(half * 4, 4)], wraw.at[0], par_sem.at[0]),
        pltpu.make_async_copy(w2.at[:, pl.ds(half * 4, 4)], wraw.at[1], par_sem.at[1]),
        pltpu.make_async_copy(b1, braw.at[0], par_sem.at[2]),
        pltpu.make_async_copy(b2, braw.at[1], par_sem.at[3]),
    ]
    for copy in params:
        copy.start()

    barrier = pltpu.get_barrier_semaphore()
    for o in OFFSETS:
        if o != (0, 0, 0):
            pl.semaphore_signal(barrier, inc=1, device_id=(batch, index(partner(o))), device_id_type=MESH)
        pl.semaphore_signal(barrier, inc=1, device_id=(other, index(partner(o))), device_id_type=MESH)
    for o in range(1, NY):
        for to in (along(o), (1 - side) * NY + (yy + o) % NY):
            pl.semaphore_signal(barrier, inc=1, device_id=(to, me), device_id_type=MESH)

    def lanes(part):
        return pl.ds(pl.multiple_of(part * HALF, 128), HALF)

    def rows16(sample, quarter, jc):
        return pl.ds(pl.multiple_of(sample * 2 * KP + quarter * 48 + jc * 16, 16), 16)

    def chunk(jc):
        return pl.ds(pl.multiple_of(jc * 16, 16), 16)

    def early(part, i):
        to = partner(OFFSETS[i])
        here = pl.ds(part * (LOCAL // 2), LOCAL // 2)
        src = send.at[0, here, rows16(to[2], to[1], 0), lanes(to[0])]
        dst = recv.at[0, me, here, chunk(0), :]
        if OFFSETS[i] == (0, 0, 0):
            return pltpu.make_async_copy(src, dst, rsem.at[0, 0])
        return pltpu.make_async_remote_copy(
            src, dst, ssem.at[0, 0], rsem.at[0, 0], device_id=(batch, index(to)), device_id_type=MESH
        )

    def inward(a, jc, i):
        to = partner(OFFSETS[i])
        src = send.at[a, :, rows16(to[2], to[1], jc), lanes(to[0])]
        dst = recv.at[a, me, :, chunk(jc), :]
        if OFFSETS[i] == (0, 0, 0):
            return pltpu.make_async_copy(src, dst, rsem.at[a, jc])
        return pltpu.make_async_remote_copy(
            src, dst, ssem.at[a, jc], rsem.at[a, jc], device_id=(batch, index(to)), device_id_type=MESH
        )

    def arrived(a, jc, region):
        pltpu.make_async_remote_copy(
            region, region, ssem.at[a, jc], rsem.at[a, jc], device_id=(batch, me), device_id_type=MESH
        ).wait_recv()

    def left(a, jc):
        region = recv.at[0, pl.ds(0, len(OFFSETS) - 1), :, pl.ds(0, 16), :]
        pltpu.make_async_remote_copy(
            region, region, ssem.at[a, jc], rsem.at[a, jc], device_id=(batch, me), device_id_type=MESH
        ).wait_send()

    def outward(jc, i):
        to = index(partner(OFFSETS[i]))
        src = gsend.at[pl.ds(to * LOCAL, LOCAL), chunk(jc), :]
        dst = grecv.at[:, rows16(core, zz, jc), lanes(half)]
        if OFFSETS[i] == (0, 0, 0):
            return pltpu.make_async_copy(src, dst, rsem.at[2, jc])
        return pltpu.make_async_remote_copy(
            src, dst, ssem.at[2, jc], rsem.at[2, jc], device_id=(batch, to), device_id_type=MESH
        )

    def longitude(a, first=0, last=LOCAL):
        table = (tf, ti)[a]

        def one(h, carry):
            slab_copy(a, h).wait()
            if a == 0:
                slab_copy(1, h).start()
            pair = slab[a, h].reshape(WIDTH * SAMPLES, CH)
            send[a, h] = dot(table[...], pair).astype(BF16)
            return carry

        lax.fori_loop(first, last, one, 0)

    tables[0].wait()
    longitude(0, 0, LOCAL // 2)
    pl.semaphore_wait(barrier, 2 * len(OFFSETS) - 1 + 2 * (NY - 1))
    for i in range(len(OFFSETS)):
        early(0, i).start()
    longitude(0, LOCAL // 2, LOCAL)
    for i in range(len(OFFSETS)):
        early(1, i).start()
    for jc in range(1, CHUNKS):
        for i in range(len(OFFSETS)):
            inward(0, jc, i).start()
    tables[1].wait()
    longitude(1)
    for jc in range(CHUNKS):
        for i in range(len(OFFSETS)):
            inward(1, jc, i).start()

    for copy in params + tables[2:]:
        copy.wait()
    row_id = lax.broadcasted_iota(jnp.int32, (BS, HALF), 0)
    col_id = lax.broadcasted_iota(jnp.int32, (BS, HALF), 1)
    for w in range(2):
        for part in range(2):
            total = jnp.zeros((8, HALF), F32)
            for n in range(4):
                place = jnp.where(row_id + n * BS == col_id, 1.0, 0.0).astype(F32)
                placed = dot(wraw[w, part, n].astype(BF16), place.astype(BF16))
                wtmp[part, n * BS : (n + 1) * BS, :] = placed.astype(BF16)
                line = jnp.broadcast_to(braw[w, part, pl.ds(half * 4 + n, 1), :], (8, BS))
                total = total + jnp.dot(line, place, precision=lax.Precision.HIGHEST, preferred_element_type=F32)
            for t in range(TILES):
                c = (2 * t + part) * 128
                bias[w, :, c : c + 128] = total[:, t * 128 : (t + 1) * 128]
        for t in range(TILES):
            for u in range(TILES):
                real = wtmp[0, t * 128 : (t + 1) * 128, u * 128 : (u + 1) * 128]
                imag = wtmp[1, t * 128 : (t + 1) * 128, u * 128 : (u + 1) * 128]
                r, c = t * 256, u * 256
                wm[w, r : r + 128, c : c + 128] = real
                wm[w, r : r + 128, c + 128 : c + 256] = imag
                wm[w, r + 128 : r + 256, c : c + 128] = -imag
                wm[w, r + 128 : r + 256, c + 128 : c + 256] = real
    acc[...] = jnp.zeros_like(acc)
    gb[...] = jnp.zeros_like(gb)

    def gather(a, jc):
        arrived(a, jc, recv.at[a, :, :, chunk(jc), :])

        def one(l, carry):
            rows = recv[a, l, :, chunk(jc), :].astype(F32).reshape(LOCAL * 16, HALF)
            for t in range(TILES):
                scr[t, pl.ds(pl.multiple_of(l * 96, 8), 96), :] = rows[:, t * 128 : (t + 1) * 128]
            return carry

        lax.fori_loop(0, 16, one, 0)

    def column(j):
        parts = [
            jnp.concatenate([scr[t, pl.ds(q * JB + j, LAT, stride=16), :] for t in range(TILES)], axis=1)
            for q in range(2)
        ]
        return jnp.concatenate(parts, axis=0).astype(BF16)

    def row_block(jc, rb):
        return pl.ds(pl.multiple_of(jc * ROWS + rb * RB, 128), RB)

    def forward(jc, carry):
        gather(0, jc)

        def one(j, c):
            res = dot(l1[...], column(j))
            rows = pl.ds(pl.multiple_of(jc * ROWS + j * LAT, 32), LAT)
            for p in range(2):
                for t in range(TILES):
                    mixed[rows, (2 * t + p) * 128 : (2 * t + p + 1) * 128] = res[
                        p * LAT : (p + 1) * LAT, t * 128 : (t + 1) * 128
                    ].astype(BF16)
            return c

        lax.fori_loop(0, JB, one, 0)

        def mix(rb, c):
            rows = row_block(jc, rb)
            for t in range(TILES):
                lo, hi = WIN[t]
                cols = slice(t * 256, (t + 1) * 256)
                x = dot(mixed[rows, lo:hi], wm[0, lo:hi, cols]) + bias[0, 0:1, cols]
                c0, c1 = math.sqrt(2.0 / math.pi), 0.044715
                xx = x * x
                th = jnp.tanh(x * (c0 + (c0 * c1) * xx))
                gate = 0.5 + 0.5 * th
                hidden[rows, cols] = (x * gate).astype(BF16)
                rise = (0.5 * x) * (1.0 - th * th) * (c0 + (3.0 * c0 * c1) * xx)
                slope[rows, cols] = (gate + rise).astype(BF16)
            for t in range(TILES):
                lo, hi = WIN[t]
                cols = slice(t * 256, (t + 1) * 256)
                y = dot(hidden[rows, lo:hi], wm[1, lo:hi, cols]) + bias[1, 0:1, cols]
                th = jnp.tanh(4.0 * y)
                mask[rows, cols] = (th * th).astype(BF16)
            return c

        lax.fori_loop(0, 2, mix, 0)
        return carry

    lax.fori_loop(0, CHUNKS, forward, 0)

    def to_hidden(jc):
        gather(1, jc)

        def one(j, c):
            res = dot(l2[...], column(j)).astype(BF16)
            rows = pl.ds(pl.multiple_of(jc * ROWS + j * LAT, 32), LAT)
            here = pl.ds(pl.multiple_of(j * LAT, 32), LAT)
            for p in range(2):
                for t in range(TILES):
                    cols = slice((2 * t + p) * 128, (2 * t + p + 1) * 128)
                    part = res[p * LAT : (p + 1) * LAT, t * 128 : (t + 1) * 128].astype(F32)
                    dsec[here, cols] = (part * mask[rows, cols].astype(F32)).astype(BF16)
            return c

        lax.fori_loop(0, JB, one, 0)

        def mix(rb, c):
            rows = row_block(jc, rb)
            here = pl.ds(pl.multiple_of(rb * RB, 128), RB)
            for t in range(TILES):
                lo, hi = WIN[t]
                cols = slice(t * 256, (t + 1) * 256)
                d = dot_tb(dsec[here, lo:hi], wm[1, cols, lo:hi])
                dfir[here, cols] = (d * slope[rows, cols].astype(F32)).astype(BF16)
            return c

        lax.fori_loop(0, 2, mix, 0)

    def to_spectra(jc):
        def mix(rb, c):
            here = pl.ds(pl.multiple_of(rb * RB, 128), RB)
            for t in range(TILES):
                lo, hi = WIN[t]
                cols = slice(t * 256, (t + 1) * 256)
                d = dot_tb(dfir[here, lo:hi], wm[0, cols, lo:hi]).astype(BF16)
                for jl in range(JB // 2):
                    for p in range(2):
                        bmat[rb * (JB // 2) + jl, p * LAT : (p + 1) * LAT, t * 128 : (t + 1) * 128] = d[
                            jl * LAT : (jl + 1) * LAT, p * 128 : (p + 1) * 128
                        ]
            return c

        lax.fori_loop(0, 2, mix, 0)

        def last(j, c):
            res = dot(l3[...], bmat[j])
            for q in range(2):
                for t in range(TILES):
                    scr[t, pl.ds(q * JB + j, LAT, stride=16), :] = res[
                        q * LAT : (q + 1) * LAT, t * 128 : (t + 1) * 128
                    ]
            return c

        lax.fori_loop(0, JB, last, 0)

        def pack(l, c):
            for t in range(TILES):
                part = scr[t, pl.ds(pl.multiple_of(l * 96, 8), 96), :]
                gsend[pl.ds(l * LOCAL, LOCAL), chunk(jc), t * 128 : (t + 1) * 128] = part.astype(BF16).reshape(
                    LOCAL, 16, 128
                )
            return c

        lax.fori_loop(0, 16, pack, 0)

    def to_weights(jc):
        here = pl.ds(pl.multiple_of(jc * ROWS, 128), ROWS)
        for t in range(TILES):
            lo, hi = WIN[t]
            cols = slice(t * 256, (t + 1) * 256)
            acc[1, cols, lo:hi] += dot_ta(hidden[here, cols], dsec[:, lo:hi])
            acc[0, cols, lo:hi] += dot_ta(mixed[here, cols], dfir[:, lo:hi])
        ones = jnp.ones((16, ROWS), BF16)
        gb[0] += dot(ones, dfir[...])[0:8]
        gb[1] += dot(ones, dsec[...])[0:8]

    def backward(jc, carry):
        to_hidden(jc)
        to_spectra(jc)

        @pl.when(jc < 1)
        def _():
            for i in range(len(OFFSETS)):
                outward(jc, i).start()

        to_weights(jc)
        return carry

    lax.fori_loop(0, CHUNKS - 1, backward, 0)
    to_hidden(CHUNKS - 1)
    to_weights(CHUNKS - 1)

    lane = lax.broadcasted_iota(jnp.int32, (BS, 128), 1)
    for w in range(2):
        for part in range(2):
            for t in range(TILES):

                def block(n):
                    found = []
                    for u, lo, hi in PIECES[n]:
                        r, c = u * 256, t * 256
                        top = acc[w, r + lo : r + hi, c + part * 128 : c + (part + 1) * 128]
                        low = acc[w, r + 128 + lo : r + 128 + hi, c + (1 - part) * 128 : c + (2 - part) * 128]
                        found.append(top + low if part == 0 else top - low)
                    return found[0] if len(found) == 1 else jnp.concatenate(found, axis=0)

                tile = jnp.where(lane < 96 - 32 * t, block(t), block(t + 1)).astype(BF16)
                for i in range(3):
                    u = ((w * 2 + part) * TILES + t) * 3 + i
                    packed[u // UNITS, u % UNITS] = tile[i * 32 : (i + 1) * 32]
    row = lax.broadcasted_iota(jnp.int32, (32, 128), 0)
    lines = jnp.zeros((32, 128), F32)
    for w in range(2):
        for part in range(2):
            for t in range(TILES):
                line = gb[w, 0:1, (2 * t + part) * 128 : (2 * t + part + 1) * 128]
                lines = jnp.where(row == (w * 2 + part) * TILES + t, jnp.broadcast_to(line, (32, 128)), lines)
    packed[7, 1] = lines.astype(BF16)
    for u in range(2, UNITS):
        packed[7, u] = jnp.zeros((32, 128), BF16)

    def share(o):
        return pltpu.make_async_remote_copy(
            packed.at[(batch + o) % BATCH], parts.at[batch], rs_s.at[o], rs_r.at[o],
            device_id=((batch + o) % BATCH, me), device_id_type=MESH,
        )

    for o in range(1, BATCH):
        share(o).start()
    back = [(jc, i) for jc in range(1, CHUNKS) for i in range(len(OFFSETS))]
    for jc, i in back[:CUTS[0]]:
        outward(jc, i).start()
    to_spectra(CHUNKS - 1)
    parts[batch] = packed[batch]
    for o in range(1, BATCH):
        dst = parts.at[(batch + BATCH - o) % BATCH]
        pltpu.make_async_remote_copy(
            dst, dst, rs_s.at[o], rs_r.at[o], device_id=(batch, me), device_id_type=MESH
        ).wait_recv()
    total = parts[0].astype(F32)
    for o in range(1, BATCH):
        total = total + parts[o].astype(F32)
    shares[...] = total.astype(BF16)

    mine = me % 8

    def to_reducer(g):
        return pltpu.make_async_remote_copy(
            shares.at[g], pieces.at[mine], sum_s.at[g], sum_r.at[mine],
            device_id=(batch, half * 8 + g), device_id_type=MESH,
        )

    def to_all(i, far):
        return pltpu.make_async_remote_copy(
            done.at[side, half, mine], done.at[side, half, mine], all_s.at[i, far], all_r.at[side, half, mine],
            device_id=((batch, other)[far], index(partner(OFFSETS[i]))), device_id_type=MESH,
        )

    listeners = [(i, far) for i, o in enumerate(OFFSETS) for far in range(2) if (o, far) != ((0, 0, 0), 0)]
    for g in range(UNITS):

        @pl.when(mine != g)
        def _(g=g):
            to_reducer(g).start()

    for jc, i in back[CUTS[0] : CUTS[1]]:
        outward(jc, i).start()

    @pl.when(mine < UNITS)
    def _():
        pieces[mine] = shares[mine]
        for g in range(8):

            @pl.when(mine != g)
            def _(g=g):
                dst = pieces.at[g]
                pltpu.make_async_remote_copy(
                    dst, dst, sum_s.at[0], sum_r.at[g], device_id=(batch, me), device_id_type=MESH
                ).wait_recv()

        whole = pieces[0].astype(F32)
        for g in range(1, 8):
            whole = whole + pieces[g].astype(F32)
        samples = SAMPLES * 2 * NY
        done[side, half, mine] = (whole * (1.0 / math.sqrt(samples * LAT * (WIDTH // 2 + 1)))).astype(BF16)
        for i, far in listeners:
            to_all(i, far).start()

    for jc, i in back[CUTS[1] : CUTS[2]]:
        outward(jc, i).start()

    for sd in range(2):
        for hf in range(2):
            for g in range(UNITS):

                @pl.when((side != sd) | (half != hf) | (mine != g))
                def _(sd=sd, hf=hf, g=g):
                    dst = done.at[sd, hf, g]
                    pltpu.make_async_remote_copy(
                        dst, dst, all_s.at[0, 0], all_r.at[sd, hf, g], device_id=(batch, me), device_id_type=MESH
                    ).wait_recv()

    def gathered(o):
        return pltpu.make_async_remote_copy(
            done.at[core], every.at[yy, core], ag_s.at[o], ag_r.at[o],
            device_id=(along(o), me), device_id_type=MESH,
        )

    def passed(o):
        got = every.at[(yy + NY - o) % NY, core]
        return pltpu.make_async_remote_copy(
            got, got, pass_s.at[o], pass_r.at[o], device_id=(batch, me + 1 - 2 * core), device_id_type=MESH
        )

    for o in range(1, NY):
        gathered(o).start()
    kept = pltpu.make_async_copy(done, every.at[yy], every_sem)
    kept.start()
    for jc, i in back[CUTS[2] :]:
        outward(jc, i).start()

    for o in range(1, NY):
        dst = every.at[(yy + NY - o) % NY, core]
        pltpu.make_async_remote_copy(
            dst, dst, ag_s.at[o], ag_r.at[o], device_id=(batch, me), device_id_type=MESH
        ).wait_recv()
        passed(o).start()
    for jc in range(CHUNKS):
        arrived(2, jc, grecv.at[:, pl.ds(0, 128), :])
    for o in range(1, NY):
        dst = every.at[(yy + NY - o) % NY, 1 - core]
        pltpu.make_async_remote_copy(
            dst, dst, pass_s.at[o], pass_r.at[o], device_id=(batch, me), device_id_type=MESH
        ).wait_recv()
    kept.wait()

    for o in range(1, BATCH):
        share(o).wait_send()
    for o in range(1, NY):
        gathered(o).wait_send()
        passed(o).wait_send()
    for g in range(UNITS):

        @pl.when(mine != g)
        def _(g=g):
            to_reducer(g).wait_send()

    @pl.when(mine < UNITS)
    def _():
        for i, far in listeners:
            to_all(i, far).wait_send()

    for a in range(3):
        for jc in range(CHUNKS):
            left(a, jc)


def finish(
    every, grecv, tt, out, gw1_hbm, gb1_hbm, gw2_hbm, gb2_hbm,
    slab, pair, sums, table, gw1, gb1, gw2, gb2, in_sem, out_sem, par_sem,
):
    fetch = [pltpu.make_async_copy(tt, table, par_sem.at[0]), pltpu.make_async_copy(every, sums, par_sem.at[1])]
    fetch[1].start()
    fetch[0].start()
    for h in range(LOCAL):
        pltpu.make_async_copy(grecv.at[h], slab.at[h], in_sem.at[h]).start()
    fetch[1].wait()
    for w, gw, gbias in ((0, gw1, gb1), (1, gw2, gb2)):
        for part in range(2):
            for hf in range(2):
                tiles, lines = [], []
                for t in range(TILES):
                    k = (w * 2 + part) * TILES + t
                    found = [sums[u // UNITS % NY, u // UNITS // NY, hf, u % UNITS] for u in range(3 * k, 3 * k + 3)]
                    tiles.append(jnp.concatenate(found, axis=0).astype(F32))
                    lines.append(jnp.broadcast_to(sums[3, 1, hf, 1].astype(F32)[k : k + 1], (8, 128)))

                def blocks(x, n):
                    if n == 0:
                        return x[0][:, :BS]
                    if n == 3:
                        return pltpu.roll(x[2], BS, 1)[:, :BS]
                    return pltpu.roll(jnp.concatenate(x[n - 1 : n + 1], axis=1), 128 + 32 * n, 1)[:, :BS]

                for n in range(4):
                    gw[part, hf * 4 + n] = blocks(tiles, n)
                    gbias[part, hf * 4 + n : hf * 4 + n + 1, :] = blocks(lines, n)[0:1]
    outs = [
        pltpu.make_async_copy(src, dst, par_sem.at[2 + i])
        for i, (src, dst) in enumerate(((gw1, gw1_hbm), (gb1, gb1_hbm), (gw2, gw2_hbm), (gb2, gb2_hbm)))
    ]
    for copy in outs:
        copy.start()
    fetch[0].wait()

    def one(h, carry):
        pltpu.make_async_copy(grecv.at[h], slab.at[h], in_sem.at[h]).wait()
        pair[h] = dot(table[...], slab[h]).astype(BF16).reshape(WIDTH, SAMPLES, CH)
        pltpu.make_async_copy(pair.at[h], out.at[h], out_sem.at[h]).start()
        return carry

    lax.fori_loop(0, LOCAL, one, 0)
    for copy in outs:
        copy.wait()
    for h in range(LOCAL):
        pltpu.make_async_copy(pair.at[h], out.at[h], out_sem.at[h]).wait()


def local(field, cotangent, weight_one, bias_one, weight_two, bias_two):
    tf, ti = lon_tables()
    tt = np.ascontiguousarray(tf.T)
    l1, l2, l3 = lat_tables()
    hbm = pl.BlockSpec(memory_space=pl.ANY)
    n_off = len(OFFSETS)

    def pairs(x):
        return x.transpose(1, 2, 0, 3)

    grecv, every = pl.pallas_call(
        kernel,
        name="afno_backward",
        out_shape=(
            jax.ShapeDtypeStruct((LOCAL, SAMPLES * 2 * KP, CH), BF16),
            jax.ShapeDtypeStruct((NY, 2, 2, UNITS, 32, 128), BF16),
        ),
        in_specs=[hbm] * 11,
        out_specs=(hbm, hbm),
        scratch_shapes=[
            pltpu.VMEM((2, LOCAL, WIDTH, SAMPLES, CH), BF16),
            pltpu.VMEM((2, LOCAL, SAMPLES * 2 * KP, CH), BF16),
            pltpu.VMEM((2, 16, LOCAL, 2 * QUARTER, HALF), BF16),
            pltpu.VMEM((LAT, 2 * QUARTER, HALF), BF16),
            pltpu.VMEM((CHUNKS * ROWS, CH), BF16),
            pltpu.VMEM((CHUNKS * ROWS, CH), BF16),
            pltpu.VMEM((CHUNKS * ROWS, CH), BF16),
            pltpu.VMEM((CHUNKS * ROWS, CH), BF16),
            pltpu.VMEM((ROWS, CH), BF16),
            pltpu.VMEM((ROWS, CH), BF16),
            pltpu.VMEM((TILES, LAT * 16 + 16, 128), F32),
            pltpu.VMEM((JB, 2 * LAT, HALF), BF16),
            pltpu.VMEM((2, CH, CH), BF16),
            pltpu.VMEM((2, HALF, HALF), BF16),
            pltpu.VMEM((2, 8, CH), F32),
            pltpu.VMEM((2, CH, CH), F32),
            pltpu.VMEM((2, 8, CH), F32),
            pltpu.VMEM((2, 2, 4, BS, BS), F32),
            pltpu.VMEM((2, 2, 8, BS), F32),
            pltpu.VMEM((BATCH, UNITS, 32, 128), BF16),
            pltpu.VMEM((BATCH, UNITS, 32, 128), BF16),
            pltpu.VMEM((UNITS, 32, 128), BF16),
            pltpu.VMEM((8, 32, 128), BF16),
            pltpu.VMEM((2, 2, UNITS, 32, 128), BF16),
            pltpu.VMEM(tf.shape, BF16),
            pltpu.VMEM(ti.shape, BF16),
            pltpu.VMEM(l1.shape, BF16),
            pltpu.VMEM(l2.shape, BF16),
            pltpu.VMEM(l3.shape, BF16),
            pltpu.SemaphoreType.DMA((5,)),
            pltpu.SemaphoreType.DMA((2, LOCAL)),
            pltpu.SemaphoreType.DMA,
            pltpu.SemaphoreType.DMA((4,)),
            pltpu.SemaphoreType.DMA((3, CHUNKS)),
            pltpu.SemaphoreType.DMA((3, CHUNKS)),
            pltpu.SemaphoreType.DMA((BATCH,)),
            pltpu.SemaphoreType.DMA((BATCH,)),
            pltpu.SemaphoreType.DMA((UNITS,)),
            pltpu.SemaphoreType.DMA((8,)),
            pltpu.SemaphoreType.DMA((n_off, 2)),
            pltpu.SemaphoreType.DMA((2, 2, UNITS)),
            pltpu.SemaphoreType.DMA((NY,)),
            pltpu.SemaphoreType.DMA((NY,)),
            pltpu.SemaphoreType.DMA((NY,)),
            pltpu.SemaphoreType.DMA((NY,)),
        ],
        compiler_params=pltpu.CompilerParams(
            collective_id=0, has_side_effects=True, vmem_limit_bytes=62 * 1024 * 1024
        ),
        cost_estimate=pl.CostEstimate(flops=10**10, bytes_accessed=10**7, transcendentals=4 * 10**6),
    )(pairs(field), pairs(cotangent), weight_one, bias_one, weight_two, bias_two, tf, ti, l1, l2, l3)

    wshape, bshape = weight_one.shape, bias_one.shape
    field_grad, *rest = pl.pallas_call(
        finish,
        name="finish",
        out_shape=(
            jax.ShapeDtypeStruct((LOCAL, WIDTH, SAMPLES, CH), BF16),
            jax.ShapeDtypeStruct(wshape, F32),
            jax.ShapeDtypeStruct(bshape, F32),
            jax.ShapeDtypeStruct(wshape, F32),
            jax.ShapeDtypeStruct(bshape, F32),
        ),
        in_specs=[hbm] * 3,
        out_specs=[hbm] * 5,
        scratch_shapes=[
            pltpu.VMEM(grecv.shape, BF16),
            pltpu.VMEM((LOCAL, WIDTH, SAMPLES, CH), BF16),
            pltpu.VMEM(every.shape, BF16),
            pltpu.VMEM(tt.shape, BF16),
            pltpu.VMEM(wshape, F32),
            pltpu.VMEM(bshape, F32),
            pltpu.VMEM(wshape, F32),
            pltpu.VMEM(bshape, F32),
            pltpu.SemaphoreType.DMA((LOCAL,)),
            pltpu.SemaphoreType.DMA((LOCAL,)),
            pltpu.SemaphoreType.DMA((6,)),
        ],
        compiler_params=pltpu.CompilerParams(vmem_limit_bytes=62 * 1024 * 1024),
        cost_estimate=pl.CostEstimate(flops=2 * 10**9, bytes_accessed=8 * 10**6, transcendentals=0),
    )(every, grecv, tt)
    return (field_grad.transpose(2, 0, 1, 3), *rest)


def solution(mesh):
    in_specs = (P("batch", "lat", None, None), P("batch", "lat", None, None), P(), P(), P(), P())
    out_specs = (P("batch", "lat", None, None), P(), P(), P(), P())
    return jax.shard_map(local, mesh=mesh, in_specs=in_specs, out_specs=out_specs, check_vma=False)
```

```python
import functools
import math

import jax
import jax.numpy as jnp
import numpy as np
from jax import lax
from jax.experimental import pallas as pl
from jax.experimental.pallas import tpu as pltpu
from jax.sharding import PartitionSpec as P

MESH = pl.DeviceIdType.MESH
F32, BF16 = jnp.float32, jnp.bfloat16
NY = 4
BATCH = 2 * NY
UNITS = 5
KP = 96
QUARTER = 24
JB = 8
CHUNKS = QUARTER // JB
HALF = 384
TILES = HALF // 128
LOCAL = 6
SAMPLES = 2
LAT = 96
WIDTH = 180
CH = 768
BS = 96
ROWS = JB * LAT
RB = ROWS // 2
OFFSETS = [(dx, dz, dc) for dz in (1, 3, 2, 0) for dx in (1, 0) for dc in (1, 0)]
CUTS = (12, 20, 26)
WIN = [(0, 512), (0, 768), (256, 768)]
PIECES = [[(0, 0, 96)], [(0, 96, 128), (1, 0, 64)], [(1, 64, 128), (2, 0, 32)], [(2, 32, 128)]]


def lon_tables():
    wpos, kpos = np.arange(WIDTH), np.arange(KP)
    angle = (wpos[:, None] * kpos[None, :] % WIDTH).astype(np.float32) * np.float32(2.0 * math.pi / WIDTH)
    valid = (kpos <= WIDTH // 2).astype(np.float32)[None, :]
    factor = np.float32(1.0 / math.sqrt(WIDTH))
    cosine, sine = np.cos(angle) * valid * factor, np.sin(angle) * valid * factor
    weight = np.where((kpos == 0) | (kpos == WIDTH // 2), 1.0, 2.0).astype(np.float32)[None, :]

    def rows(real, imag):
        both = np.stack([real.T, imag.T]).reshape(2, 4, CHUNKS, JB, WIDTH)
        return both.transpose(1, 2, 0, 3, 4).reshape(2 * KP, WIDTH).astype(BF16)

    def paired(table):
        both = np.zeros((SAMPLES, 2 * KP, WIDTH, SAMPLES), BF16)
        for s in range(SAMPLES):
            both[s, :, :, s] = table
        return both.reshape(SAMPLES * 2 * KP, WIDTH * SAMPLES)

    return paired(rows(cosine, -sine)), paired(rows(cosine * weight, -sine * weight))


def lat_tables():
    pos = np.arange(LAT)
    angle = (pos[:, None] * pos[None, :] % LAT).astype(np.float32) * np.float32(2.0 * math.pi / LAT)
    factor = np.float32(1.0 / math.sqrt(LAT))
    cosine = np.cos(angle) * factor

    def real_form(sign):
        sine = np.sin(angle) * np.float32(factor * sign)
        return np.stack([np.stack([cosine, -sine], -1), np.stack([sine, cosine], -1)], 1).astype(BF16)

    fwd = real_form(-1.0).transpose(1, 0, 3, 2).reshape(2 * LAT, 2 * LAT)
    inv = real_form(1.0).transpose(3, 2, 1, 0).reshape(2 * LAT, 2 * LAT)
    return fwd, inv, np.ascontiguousarray(fwd.T)


def dot(a, b):
    return jnp.dot(a, b, preferred_element_type=F32)


def dot_tb(a, b):
    return lax.dot_general(a, b, (((1,), (1,)), ((), ())), preferred_element_type=F32)


def dot_ta(a, b):
    return lax.dot_general(a, b, (((0,), (0,)), ((), ())), preferred_element_type=F32)


def kernel(
    field, cot, w1, b1, w2, b2, tf_hbm, ti_hbm, l1_hbm, l2_hbm, l3_hbm,
    grecv, every,
    slab, send, recv, gsend, mixed, hidden, slope, mask, dsec, dfir, scr, bmat, wm, wtmp, bias, acc, gb,
    wraw, braw, packed, parts, shares, pieces, done, whole_ref, tf, ti, l1, l2, l3,
    table_sem, slab_sem, every_sem, par_sem, ssem, rsem, rs_s, rs_r, sum_s, sum_r, all_s, all_r, ag_s, ag_r, pass_s, pass_r,
):
    batch, me = lax.axis_index("batch"), lax.axis_index("lat")
    half, zz, core = me // 8, (me // 2) % 4, me % 2
    side, yy = batch // NY, batch % NY
    other = (1 - side) * NY + yy

    def along(o):
        return side * NY + (yy + o) % NY

    def partner(o):
        dx, dz, dc = o
        return (half + dx) % 2, (zz + dz) % 4, (core + dc) % 2

    def index(part):
        return part[0] * 8 + part[1] * 2 + part[2]

    def slab_copy(a, h):
        return pltpu.make_async_copy((field, cot)[a].at[h], slab.at[a, h], slab_sem.at[a, h])

    tables = [
        pltpu.make_async_copy(src, dst, table_sem.at[i])
        for i, (src, dst) in enumerate(((tf_hbm, tf), (ti_hbm, ti), (l1_hbm, l1), (l2_hbm, l2), (l3_hbm, l3)))
    ]
    tables[0].start()
    for h in range(LOCAL):
        slab_copy(0, h).start()
    for copy in tables[1:]:
        copy.start()
    params = [
        pltpu.make_async_copy(w1.at[:, pl.ds(half * 4, 4)], wraw.at[0], par_sem.at[0]),
        pltpu.make_async_copy(w2.at[:, pl.ds(half * 4, 4)], wraw.at[1], par_sem.at[1]),
        pltpu.make_async_copy(b1, braw.at[0], par_sem.at[2]),
        pltpu.make_async_copy(b2, braw.at[1], par_sem.at[3]),
    ]
    for copy in params:
        copy.start()

    barrier = pltpu.get_barrier_semaphore()
    for o in OFFSETS:
        if o != (0, 0, 0):
            pl.semaphore_signal(barrier, inc=1, device_id=(batch, index(partner(o))), device_id_type=MESH)
        pl.semaphore_signal(barrier, inc=1, device_id=(other, index(partner(o))), device_id_type=MESH)
    for o in range(1, NY):
        for to in (along(o), (1 - side) * NY + (yy + o) % NY):
            pl.semaphore_signal(barrier, inc=1, device_id=(to, me), device_id_type=MESH)

    def lanes(part):
        return pl.ds(pl.multiple_of(part * HALF, 128), HALF)

    def rows16(sample, quarter, jc):
        return pl.ds(pl.multiple_of(sample * 2 * KP + quarter * 48 + jc * 16, 16), 16)

    def chunk(jc):
        return pl.ds(pl.multiple_of(jc * 16, 16), 16)

    def early(part, i):
        to = partner(OFFSETS[i])
        here = pl.ds(part * (LOCAL // 2), LOCAL // 2)
        src = send.at[0, here, rows16(to[2], to[1], 0), lanes(to[0])]
        dst = recv.at[0, me, here, chunk(0), :]
        if OFFSETS[i] == (0, 0, 0):
            return pltpu.make_async_copy(src, dst, rsem.at[0, 0])
        return pltpu.make_async_remote_copy(
            src, dst, ssem.at[0, 0], rsem.at[0, 0], device_id=(batch, index(to)), device_id_type=MESH
        )

    def inward(a, jc, i):
        to = partner(OFFSETS[i])
        src = send.at[a, :, rows16(to[2], to[1], jc), lanes(to[0])]
        dst = recv.at[a, me, :, chunk(jc), :]
        if OFFSETS[i] == (0, 0, 0):
            return pltpu.make_async_copy(src, dst, rsem.at[a, jc])
        return pltpu.make_async_remote_copy(
            src, dst, ssem.at[a, jc], rsem.at[a, jc], device_id=(batch, index(to)), device_id_type=MESH
        )

    def arrived(a, jc, region):
        pltpu.make_async_remote_copy(
            region, region, ssem.at[a, jc], rsem.at[a, jc], device_id=(batch, me), device_id_type=MESH
        ).wait_recv()

    def left(a, jc):
        region = recv.at[0, pl.ds(0, len(OFFSETS) - 1), :, pl.ds(0, 16), :]
        pltpu.make_async_remote_copy(
            region, region, ssem.at[a, jc], rsem.at[a, jc], device_id=(batch, me), device_id_type=MESH
        ).wait_send()

    def outward(jc, i):
        to = index(partner(OFFSETS[i]))
        src = gsend.at[pl.ds(to * LOCAL, LOCAL), chunk(jc), :]
        dst = grecv.at[:, rows16(core, zz, jc), lanes(half)]
        if OFFSETS[i] == (0, 0, 0):
            return pltpu.make_async_copy(src, dst, rsem.at[2, jc])
        return pltpu.make_async_remote_copy(
            src, dst, ssem.at[2, jc], rsem.at[2, jc], device_id=(batch, to), device_id_type=MESH
        )

    def longitude(a, first=0, last=LOCAL):
        table = (tf, ti)[a]

        def one(h, carry):
            slab_copy(a, h).wait()
            if a == 0:
                slab_copy(1, h).start()
            pair = slab[a, h].reshape(WIDTH * SAMPLES, CH)
            send[a, h] = dot(table[...], pair).astype(BF16)
            return carry

        lax.fori_loop(first, last, one, 0)

    tables[0].wait()
    longitude(0, 0, LOCAL // 2)
    pl.semaphore_wait(barrier, 2 * len(OFFSETS) - 1 + 2 * (NY - 1))
    for i in range(len(OFFSETS)):
        early(0, i).start()
    longitude(0, LOCAL // 2, LOCAL)
    for i in range(len(OFFSETS)):
        early(1, i).start()
    for jc in range(1, CHUNKS):
        for i in range(len(OFFSETS)):
            inward(0, jc, i).start()
    tables[1].wait()
    longitude(1)
    for jc in range(CHUNKS):
        for i in range(len(OFFSETS)):
            inward(1, jc, i).start()

    for copy in params + tables[2:]:
        copy.wait()
    row_id = lax.broadcasted_iota(jnp.int32, (BS, HALF), 0)
    col_id = lax.broadcasted_iota(jnp.int32, (BS, HALF), 1)
    for w in range(2):
        for part in range(2):
            total = jnp.zeros((8, HALF), F32)
            for n in range(4):
                place = jnp.where(row_id + n * BS == col_id, 1.0, 0.0).astype(F32)
                placed = dot(wraw[w, part, n].astype(BF16), place.astype(BF16))
                wtmp[part, n * BS : (n + 1) * BS, :] = placed.astype(BF16)
                line = jnp.broadcast_to(braw[w, part, pl.ds(half * 4 + n, 1), :], (8, BS))
                total = total + jnp.dot(line, place, precision=lax.Precision.HIGHEST, preferred_element_type=F32)
            for t in range(TILES):
                c = (2 * t + part) * 128
                bias[w, :, c : c + 128] = total[:, t * 128 : (t + 1) * 128]
        for t in range(TILES):
            for u in range(TILES):
                real = wtmp[0, t * 128 : (t + 1) * 128, u * 128 : (u + 1) * 128]
                imag = wtmp[1, t * 128 : (t + 1) * 128, u * 128 : (u + 1) * 128]
                r, c = t * 256, u * 256
                wm[w, r : r + 128, c : c + 128] = real
                wm[w, r : r + 128, c + 128 : c + 256] = imag
                wm[w, r + 128 : r + 256, c : c + 128] = -imag
                wm[w, r + 128 : r + 256, c + 128 : c + 256] = real
    acc[...] = jnp.zeros_like(acc)
    gb[...] = jnp.zeros_like(gb)

    def gather(a, jc):
        arrived(a, jc, recv.at[a, :, :, chunk(jc), :])

        def one(l, carry):
            rows = recv[a, l, :, chunk(jc), :].astype(F32).reshape(LOCAL * 16, HALF)
            for t in range(TILES):
                scr[t, pl.ds(pl.multiple_of(l * 96, 8), 96), :] = rows[:, t * 128 : (t + 1) * 128]
            return carry

        lax.fori_loop(0, 16, one, 0)

    def column(j):
        parts = [
            jnp.concatenate([scr[t, pl.ds(q * JB + j, LAT, stride=16), :] for t in range(TILES)], axis=1)
            for q in range(2)
        ]
        return jnp.concatenate(parts, axis=0).astype(BF16)

    def row_block(jc, rb):
        return pl.ds(pl.multiple_of(jc * ROWS + rb * RB, 128), RB)

    def forward(jc, carry):
        gather(0, jc)

        def one(j, c):
            res = dot(l1[...], column(j))
            rows = pl.ds(pl.multiple_of(jc * ROWS + j * LAT, 32), LAT)
            for p in range(2):
                for t in range(TILES):
                    mixed[rows, (2 * t + p) * 128 : (2 * t + p + 1) * 128] = res[
                        p * LAT : (p + 1) * LAT, t * 128 : (t + 1) * 128
                    ].astype(BF16)
            return c

        lax.fori_loop(0, JB, one, 0)

        def mix(rb, c):
            rows = row_block(jc, rb)
            for t in range(TILES):
                lo, hi = WIN[t]
                cols = slice(t * 256, (t + 1) * 256)
                x = dot(mixed[rows, lo:hi], wm[0, lo:hi, cols]) + bias[0, 0:1, cols]
                c0, c1 = math.sqrt(2.0 / math.pi), 0.044715
                xx = x * x
                th = jnp.tanh(x * (c0 + (c0 * c1) * xx))
                gate = 0.5 + 0.5 * th
                hidden[rows, cols] = (x * gate).astype(BF16)
                rise = (0.5 * x) * (1.0 - th * th) * (c0 + (3.0 * c0 * c1) * xx)
                slope[rows, cols] = (gate + rise).astype(BF16)
            for t in range(TILES):
                lo, hi = WIN[t]
                cols = slice(t * 256, (t + 1) * 256)
                y = dot(hidden[rows, lo:hi], wm[1, lo:hi, cols]) + bias[1, 0:1, cols]
                th = jnp.tanh(4.0 * y)
                mask[rows, cols] = (th * th).astype(BF16)
            return c

        lax.fori_loop(0, 2, mix, 0)
        return carry

    lax.fori_loop(0, CHUNKS, forward, 0)

    def to_hidden(jc):
        gather(1, jc)

        def one(j, c):
            res = dot(l2[...], column(j)).astype(BF16)
            rows = pl.ds(pl.multiple_of(jc * ROWS + j * LAT, 32), LAT)
            here = pl.ds(pl.multiple_of(j * LAT, 32), LAT)
            for p in range(2):
                for t in range(TILES):
                    cols = slice((2 * t + p) * 128, (2 * t + p + 1) * 128)
                    part = res[p * LAT : (p + 1) * LAT, t * 128 : (t + 1) * 128].astype(F32)
                    dsec[here, cols] = (part * mask[rows, cols].astype(F32)).astype(BF16)
            return c

        lax.fori_loop(0, JB, one, 0)

        def mix(rb, c):
            rows = row_block(jc, rb)
            here = pl.ds(pl.multiple_of(rb * RB, 128), RB)
            for t in range(TILES):
                lo, hi = WIN[t]
                cols = slice(t * 256, (t + 1) * 256)
                d = dot_tb(dsec[here, lo:hi], wm[1, cols, lo:hi])
                dfir[here, cols] = (d * slope[rows, cols].astype(F32)).astype(BF16)
            return c

        lax.fori_loop(0, 2, mix, 0)

    def to_spectra(jc):
        def mix(rb, c):
            here = pl.ds(pl.multiple_of(rb * RB, 128), RB)
            for t in range(TILES):
                lo, hi = WIN[t]
                cols = slice(t * 256, (t + 1) * 256)
                d = dot_tb(dfir[here, lo:hi], wm[0, cols, lo:hi]).astype(BF16)
                for jl in range(JB // 2):
                    for p in range(2):
                        bmat[rb * (JB // 2) + jl, p * LAT : (p + 1) * LAT, t * 128 : (t + 1) * 128] = d[
                            jl * LAT : (jl + 1) * LAT, p * 128 : (p + 1) * 128
                        ]
            return c

        lax.fori_loop(0, 2, mix, 0)

        def last(j, c):
            res = dot(l3[...], bmat[j])
            for q in range(2):
                for t in range(TILES):
                    scr[t, pl.ds(q * JB + j, LAT, stride=16), :] = res[
                        q * LAT : (q + 1) * LAT, t * 128 : (t + 1) * 128
                    ]
            return c

        lax.fori_loop(0, JB, last, 0)

        def pack(l, c):
            for t in range(TILES):
                part = scr[t, pl.ds(pl.multiple_of(l * 96, 8), 96), :]
                gsend[pl.ds(l * LOCAL, LOCAL), chunk(jc), t * 128 : (t + 1) * 128] = part.astype(BF16).reshape(
                    LOCAL, 16, 128
                )
            return c

        lax.fori_loop(0, 16, pack, 0)

    def to_weights(jc):
        here = pl.ds(pl.multiple_of(jc * ROWS, 128), ROWS)
        for t in range(TILES):
            lo, hi = WIN[t]
            cols = slice(t * 256, (t + 1) * 256)
            acc[1, cols, lo:hi] += dot_ta(hidden[here, cols], dsec[:, lo:hi])
            acc[0, cols, lo:hi] += dot_ta(mixed[here, cols], dfir[:, lo:hi])
        ones = jnp.ones((16, ROWS), BF16)
        gb[0] += dot(ones, dfir[...])[0:8]
        gb[1] += dot(ones, dsec[...])[0:8]

    def backward(jc, carry):
        to_hidden(jc)
        to_spectra(jc)

        @pl.when(jc < 1)
        def _():
            for i in range(len(OFFSETS)):
                outward(jc, i).start()

        to_weights(jc)
        return carry

    lax.fori_loop(0, CHUNKS - 1, backward, 0)
    to_hidden(CHUNKS - 1)
    to_weights(CHUNKS - 1)

    lane = lax.broadcasted_iota(jnp.int32, (BS, 128), 1)
    for w in range(2):
        for part in range(2):
            for t in range(TILES):

                def block(n):
                    found = []
                    for u, lo, hi in PIECES[n]:
                        r, c = u * 256, t * 256
                        top = acc[w, r + lo : r + hi, c + part * 128 : c + (part + 1) * 128]
                        low = acc[w, r + 128 + lo : r + 128 + hi, c + (1 - part) * 128 : c + (2 - part) * 128]
                        found.append(top + low if part == 0 else top - low)
                    return found[0] if len(found) == 1 else jnp.concatenate(found, axis=0)

                tile = jnp.where(lane < 96 - 32 * t, block(t), block(t + 1)).astype(BF16)
                for i in range(3):
                    u = ((w * 2 + part) * TILES + t) * 3 + i
                    packed[u // UNITS, u % UNITS] = tile[i * 32 : (i + 1) * 32]
    row = lax.broadcasted_iota(jnp.int32, (32, 128), 0)
    lines = jnp.zeros((32, 128), F32)
    for w in range(2):
        for part in range(2):
            for t in range(TILES):
                line = gb[w, 0:1, (2 * t + part) * 128 : (2 * t + part + 1) * 128]
                lines = jnp.where(row == (w * 2 + part) * TILES + t, jnp.broadcast_to(line, (32, 128)), lines)
    packed[7, 1] = lines.astype(BF16)
    for u in range(2, UNITS):
        packed[7, u] = jnp.zeros((32, 128), BF16)

    def share(o):
        return pltpu.make_async_remote_copy(
            packed.at[(batch + o) % BATCH], parts.at[batch], rs_s, rs_r,
            device_id=((batch + o) % BATCH, me), device_id_type=MESH,
        )

    for o in range(1, BATCH):
        share(o).start()
    back = [(jc, i) for jc in range(1, CHUNKS) for i in range(len(OFFSETS))]
    for jc, i in back[:CUTS[0]]:
        outward(jc, i).start()
    to_spectra(CHUNKS - 1)
    parts[batch] = packed[batch]
    others = parts.at[pl.ds(0, BATCH - 1)]
    pltpu.make_async_remote_copy(
        others, others, rs_s, rs_r, device_id=(batch, me), device_id_type=MESH
    ).wait_recv()
    total = parts[0].astype(F32)
    for o in range(1, BATCH):
        total = total + parts[o].astype(F32)
    shares[...] = total.astype(BF16)

    mine = me % 8

    def to_reducer(g):
        return pltpu.make_async_remote_copy(
            shares.at[g], pieces.at[mine], sum_s.at[g], sum_r,
            device_id=(batch, half * 8 + g), device_id_type=MESH,
        )

    def to_all(i, far):
        return pltpu.make_async_remote_copy(
            whole_ref, done.at[side, half, mine], all_s.at[far], all_r,
            device_id=((batch, other)[far], index(partner(OFFSETS[i]))), device_id_type=MESH,
        )

    listeners = [(i, far) for i, o in enumerate(OFFSETS) for far in range(2) if (o, far) != ((0, 0, 0), 0)]
    for g in range(UNITS):

        @pl.when(mine != g)
        def _(g=g):
            to_reducer(g).start()

    for jc, i in back[CUTS[0] : CUTS[1]]:
        outward(jc, i).start()

    @pl.when(mine < UNITS)
    def _():
        pieces[mine] = shares[mine]
        others = pieces.at[pl.ds(0, 7)]
        pltpu.make_async_remote_copy(
            others, others, sum_s.at[0], sum_r, device_id=(batch, me), device_id_type=MESH
        ).wait_recv()
        whole = pieces[0].astype(F32)
        for g in range(1, 8):
            whole = whole + pieces[g].astype(F32)
        samples = SAMPLES * 2 * NY
        whole_ref[...] = (whole * (1.0 / math.sqrt(samples * LAT * (WIDTH // 2 + 1)))).astype(BF16)
        for i, far in listeners:
            to_all(i, far).start()
        pltpu.make_async_copy(whole_ref, done.at[side, half, mine], all_r).start()

    for jc, i in back[CUTS[1] : CUTS[2]]:
        outward(jc, i).start()

    pltpu.make_async_remote_copy(
        done, done, all_s.at[0], all_r, device_id=(batch, me), device_id_type=MESH
    ).wait_recv()

    def gathered(o):
        return pltpu.make_async_remote_copy(
            done.at[core], every.at[yy, core], ag_s.at[o], ag_r.at[o],
            device_id=(along(o), me), device_id_type=MESH,
        )

    def passed(o):
        got = every.at[(yy + NY - o) % NY, core]
        return pltpu.make_async_remote_copy(
            got, got, pass_s.at[o], pass_r.at[o], device_id=(batch, me + 1 - 2 * core), device_id_type=MESH
        )

    for o in range(1, NY):
        gathered(o).start()
    kept = pltpu.make_async_copy(done, every.at[yy], every_sem)
    kept.start()
    for jc, i in back[CUTS[2] :]:
        outward(jc, i).start()

    for o in range(1, NY):
        dst = every.at[(yy + NY - o) % NY, core]
        pltpu.make_async_remote_copy(
            dst, dst, ag_s.at[o], ag_r.at[o], device_id=(batch, me), device_id_type=MESH
        ).wait_recv()
        passed(o).start()
    for jc in range(CHUNKS):
        arrived(2, jc, grecv.at[:, pl.ds(0, 128), :])
    for o in range(1, NY):
        dst = every.at[(yy + NY - o) % NY, 1 - core]
        pltpu.make_async_remote_copy(
            dst, dst, pass_s.at[o], pass_r.at[o], device_id=(batch, me), device_id_type=MESH
        ).wait_recv()
    kept.wait()

    sent = packed.at[pl.ds(0, BATCH - 1)]
    pltpu.make_async_remote_copy(
        sent, sent, rs_s, rs_r, device_id=(batch, me), device_id_type=MESH
    ).wait_send()
    for o in range(1, NY):
        gathered(o).wait_send()
        passed(o).wait_send()
    for g in range(UNITS):

        @pl.when(mine != g)
        def _(g=g):
            to_reducer(g).wait_send()

    @pl.when(mine < UNITS)
    def _():
        for far in range(2):
            sent = mixed.at[pl.ds(0, 32 * (len(OFFSETS) - 1 + far)), pl.ds(0, 128)]
            pltpu.make_async_remote_copy(
                sent, sent, all_s.at[far], all_r, device_id=(batch, me), device_id_type=MESH
            ).wait_send()

    for a in range(3):
        for jc in range(CHUNKS):
            left(a, jc)


def finish(
    every, grecv, tt, out, gw1_hbm, gb1_hbm, gw2_hbm, gb2_hbm,
    slab, pair, sums, table, gw1, gb1, gw2, gb2, in_sem, out_sem, par_sem,
):
    fetch = [pltpu.make_async_copy(tt, table, par_sem.at[0]), pltpu.make_async_copy(every, sums, par_sem.at[1])]
    fetch[1].start()
    fetch[0].start()
    for h in range(LOCAL):
        pltpu.make_async_copy(grecv.at[h], slab.at[h], in_sem.at[h]).start()
    fetch[1].wait()
    for w, gw, gbias in ((0, gw1, gb1), (1, gw2, gb2)):
        for part in range(2):
            for hf in range(2):
                tiles, lines = [], []
                for t in range(TILES):
                    k = (w * 2 + part) * TILES + t
                    found = [sums[u // UNITS % NY, u // UNITS // NY, hf, u % UNITS] for u in range(3 * k, 3 * k + 3)]
                    tiles.append(jnp.concatenate(found, axis=0).astype(F32))
                    lines.append(jnp.broadcast_to(sums[3, 1, hf, 1].astype(F32)[k : k + 1], (8, 128)))

                def blocks(x, n):
                    if n == 0:
                        return x[0][:, :BS]
                    if n == 3:
                        return pltpu.roll(x[2], BS, 1)[:, :BS]
                    return pltpu.roll(jnp.concatenate(x[n - 1 : n + 1], axis=1), 128 + 32 * n, 1)[:, :BS]

                for n in range(4):
                    gw[part, hf * 4 + n] = blocks(tiles, n)
                    gbias[part, hf * 4 + n : hf * 4 + n + 1, :] = blocks(lines, n)[0:1]
    outs = [
        pltpu.make_async_copy(src, dst, par_sem.at[2 + i])
        for i, (src, dst) in enumerate(((gw1, gw1_hbm), (gb1, gb1_hbm), (gw2, gw2_hbm), (gb2, gb2_hbm)))
    ]
    for copy in outs:
        copy.start()
    fetch[0].wait()

    def one(h, carry):
        pltpu.make_async_copy(grecv.at[h], slab.at[h], in_sem.at[h]).wait()
        pair[h] = dot(table[...], slab[h]).astype(BF16).reshape(WIDTH, SAMPLES, CH)
        pltpu.make_async_copy(pair.at[h], out.at[h], out_sem.at[h]).start()
        return carry

    lax.fori_loop(0, LOCAL, one, 0)
    for copy in outs:
        copy.wait()
    for h in range(LOCAL):
        pltpu.make_async_copy(pair.at[h], out.at[h], out_sem.at[h]).wait()


def local(field, cotangent, weight_one, bias_one, weight_two, bias_two):
    tf, ti = lon_tables()
    tt = np.ascontiguousarray(tf.T)
    l1, l2, l3 = lat_tables()
    hbm = pl.BlockSpec(memory_space=pl.ANY)

    def pairs(x):
        return x.transpose(1, 2, 0, 3)

    grecv, every = pl.pallas_call(
        kernel,
        name="afno_backward",
        out_shape=(
            jax.ShapeDtypeStruct((LOCAL, SAMPLES * 2 * KP, CH), BF16),
            jax.ShapeDtypeStruct((NY, 2, 2, UNITS, 32, 128), BF16),
        ),
        in_specs=[hbm] * 11,
        out_specs=(hbm, hbm),
        scratch_shapes=[
            pltpu.VMEM((2, LOCAL, WIDTH, SAMPLES, CH), BF16),
            pltpu.VMEM((2, LOCAL, SAMPLES * 2 * KP, CH), BF16),
            pltpu.VMEM((2, 16, LOCAL, 2 * QUARTER, HALF), BF16),
            pltpu.VMEM((LAT, 2 * QUARTER, HALF), BF16),
            pltpu.VMEM((CHUNKS * ROWS, CH), BF16),
            pltpu.VMEM((CHUNKS * ROWS, CH), BF16),
            pltpu.VMEM((CHUNKS * ROWS, CH), BF16),
            pltpu.VMEM((CHUNKS * ROWS, CH), BF16),
            pltpu.VMEM((ROWS, CH), BF16),
            pltpu.VMEM((ROWS, CH), BF16),
            pltpu.VMEM((TILES, LAT * 16 + 16, 128), F32),
            pltpu.VMEM((JB, 2 * LAT, HALF), BF16),
            pltpu.VMEM((2, CH, CH), BF16),
            pltpu.VMEM((2, HALF, HALF), BF16),
            pltpu.VMEM((2, 8, CH), F32),
            pltpu.VMEM((2, CH, CH), F32),
            pltpu.VMEM((2, 8, CH), F32),
            pltpu.VMEM((2, 2, 4, BS, BS), F32),
            pltpu.VMEM((2, 2, 8, BS), F32),
            pltpu.VMEM((BATCH, UNITS, 32, 128), BF16),
            pltpu.VMEM((BATCH, UNITS, 32, 128), BF16),
            pltpu.VMEM((UNITS, 32, 128), BF16),
            pltpu.VMEM((8, 32, 128), BF16),
            pltpu.VMEM((2, 2, UNITS, 32, 128), BF16),
            pltpu.VMEM((32, 128), BF16),
            pltpu.VMEM(tf.shape, BF16),
            pltpu.VMEM(ti.shape, BF16),
            pltpu.VMEM(l1.shape, BF16),
            pltpu.VMEM(l2.shape, BF16),
            pltpu.VMEM(l3.shape, BF16),
            pltpu.SemaphoreType.DMA((5,)),
            pltpu.SemaphoreType.DMA((2, LOCAL)),
            pltpu.SemaphoreType.DMA,
            pltpu.SemaphoreType.DMA((4,)),
            pltpu.SemaphoreType.DMA((3, CHUNKS)),
            pltpu.SemaphoreType.DMA((3, CHUNKS)),
            pltpu.SemaphoreType.DMA,
            pltpu.SemaphoreType.DMA,
            pltpu.SemaphoreType.DMA((UNITS,)),
            pltpu.SemaphoreType.DMA,
            pltpu.SemaphoreType.DMA((2,)),
            pltpu.SemaphoreType.DMA,
            pltpu.SemaphoreType.DMA((NY,)),
            pltpu.SemaphoreType.DMA((NY,)),
            pltpu.SemaphoreType.DMA((NY,)),
            pltpu.SemaphoreType.DMA((NY,)),
        ],
        compiler_params=pltpu.CompilerParams(
            collective_id=0, has_side_effects=True, vmem_limit_bytes=62 * 1024 * 1024
        ),
        cost_estimate=pl.CostEstimate(flops=10**10, bytes_accessed=10**7, transcendentals=4 * 10**6),
    )(pairs(field), pairs(cotangent), weight_one, bias_one, weight_two, bias_two, tf, ti, l1, l2, l3)

    wshape, bshape = weight_one.shape, bias_one.shape
    field_grad, *rest = pl.pallas_call(
        finish,
        name="finish",
        out_shape=(
            jax.ShapeDtypeStruct((LOCAL, WIDTH, SAMPLES, CH), BF16),
            jax.ShapeDtypeStruct(wshape, F32),
            jax.ShapeDtypeStruct(bshape, F32),
            jax.ShapeDtypeStruct(wshape, F32),
            jax.ShapeDtypeStruct(bshape, F32),
        ),
        in_specs=[hbm] * 3,
        out_specs=[hbm] * 5,
        scratch_shapes=[
            pltpu.VMEM(grecv.shape, BF16),
            pltpu.VMEM((LOCAL, WIDTH, SAMPLES, CH), BF16),
            pltpu.VMEM(every.shape, BF16),
            pltpu.VMEM(tt.shape, BF16),
            pltpu.VMEM(wshape, F32),
            pltpu.VMEM(bshape, F32),
            pltpu.VMEM(wshape, F32),
            pltpu.VMEM(bshape, F32),
            pltpu.SemaphoreType.DMA((LOCAL,)),
            pltpu.SemaphoreType.DMA((LOCAL,)),
            pltpu.SemaphoreType.DMA((6,)),
        ],
        compiler_params=pltpu.CompilerParams(vmem_limit_bytes=62 * 1024 * 1024),
        cost_estimate=pl.CostEstimate(flops=2 * 10**9, bytes_accessed=8 * 10**6, transcendentals=0),
    )(every, grecv, tt)
    return (field_grad.transpose(2, 0, 1, 3), *rest)


def solution(mesh):
    in_specs = (P("batch", "lat", None, None), P("batch", "lat", None, None), P(), P(), P(), P())
    out_specs = (P("batch", "lat", None, None), P(), P(), P(), P())
    return jax.shard_map(local, mesh=mesh, in_specs=in_specs, out_specs=out_specs, check_vma=False)
```
